128 devices in a mesh: tm: 4 (over x), video: 32 (over y, z, core).
Axes of the slice: x: 4, y: 4, z: 4, core: 2. Of those that a mesh axis runs over, the one named last changes fastest.
Arguments:
- latent: bfloat16 [4, 3, 16, 12, 128, 16], P('tm', None, None, None, 'video'), may hold values from -6 to 6
- routing: int32 [16], replicated, may hold values from 0 to 15, each once
- counts: int32 [16], replicated, may hold values from 1 to 4, as said below
- offsets: int32 [16], replicated, may hold values from 0 to 3, as said below
- in_weight: bfloat16 [3, 3, 48, 384], replicated, may hold values from -0.3125 to 0.3125
- in_bias: float32 [384], replicated, may hold values from -3 to 3
- first_gain: float32 [384], replicated, may hold values from 0.1 to 1.9
- first_weight: bfloat16 [3, 3, 1152, 384], replicated, may hold values from -0.0625 to 0.0625
- first_bias: float32 [384], replicated, may hold values from -3 to 3
- second_gain: float32 [384], replicated, may hold values from 0.1 to 1.9
- second_weight: bfloat16 [3, 3, 1152, 384], replicated, may hold values from -0.0625 to 0.0625
- second_bias: float32 [384], replicated, may hold values from -3 to 3
Outputs:
- decoded: bfloat16 [4, 3, 192, 128, 384], P('tm', None, 'video')
The draws below stay inside these ranges and needn't reach their ends.
Inputs may be any that keep to these rules, and one draw needn't show every extreme that they name: `routing`: a permutation: each video has its own decoder slot. `counts`: every video has at least one span. offsets[v] + counts[v] <= 4.
All inputs are finite; a program needn't handle non-finite values.
Results may differ from the reference program's by a relative error of at most 0.013.
Values may be sent and summed in bfloat16 or wider, within the bound.
No kernel may reach another device: no remote copies, remote signals or barrier semaphores. Data moves between devices by JAX's collectives and lax.ppermute only.
A program may use at most 384 MiB of HBM per device.

```python
import jax
import jax.numpy as jnp
from jax import lax

C = 384
Z = 16
ROWS = 3
COLS = 128
FR = 3
BANDS = 4
VPG = 2
SPANS = 4
VIDS = 16
WROWS = 12


def span_plan(key):
    pick_key, spare_key, base_key, late_key = jax.random.split(key, 4)
    full_video = jax.random.randint(pick_key, (), 0, VIDS)
    single = (full_video + 1 + jax.random.randint(spare_key, (), 0, VIDS - 1)) % VIDS
    slot_ids = jnp.arange(VIDS)
    span_counts = jax.random.randint(base_key, (VIDS,), 1, SPANS + 1)
    span_counts = jnp.where(slot_ids == full_video, SPANS, jnp.where(slot_ids == single, 1, span_counts))
    first_slots = jax.random.randint(late_key, (VIDS,), 0, SPANS - span_counts + 1)
    first_slots = jnp.where(slot_ids == single, SPANS - 1, first_slots)
    return (span_counts.astype(jnp.int32), first_slots.astype(jnp.int32))


def draw_counts(key, part):
    return span_plan(key)[0]


def draw_offsets(key, part):
    return span_plan(key)[1]


def steps_of(own_key, extent, shards, smallest, largest):
    loudness = 1.0
    for position, parts in shards:
        draws = jax.random.uniform(jax.random.fold_in(jax.random.fold_in(own_key, 6), position), (parts,), jnp.float32, smallest / len(shards), largest / len(shards))
        loudness = loudness * jnp.repeat(jnp.exp(draws), extent[position] // parts).reshape((-1,) + (1,) * (len(extent) - 1 - position))
    return loudness


def noise(rng, shape, deviation, bound, pieces=(), held_as=jnp.bfloat16):
    entries = deviation * jax.random.normal(rng, shape, jnp.float32)
    if pieces:
        entries = entries * steps_of(rng, shape, pieces, -0.22, 0.18)
    return jnp.clip(entries, -bound, bound).astype(held_as)


def setup_inputs(seed: int = 0) -> dict:
    key_list = jax.random.split(jax.random.key(seed), 13)
    latent = noise(key_list[0], (SPANS, FR, VIDS, WROWS, COLS, Z), 1.0, 6.0, ((0, 4), (4, 32)))
    routing = jax.random.permutation(key_list[1], VIDS).astype(jnp.int32)
    counts = draw_counts(jax.random.fold_in(key_list[12], 71), 0)
    offsets = draw_offsets(jax.random.fold_in(key_list[12], 71), 0)
    in_weight = noise(key_list[4], (3, 3, 3 * Z, C), (27 * Z) ** -0.5, 0.3125)
    in_bias = noise(key_list[5], (C,), 0.5, 3.0, (), jnp.float32)
    first_gain = jnp.clip(1.0 + 0.18 * jax.random.normal(key_list[6], (C,), jnp.float32), 0.1, 1.9)
    first_weight = noise(key_list[7], (3, 3, 3 * C, C), (27 * C) ** -0.5, 0.0625)
    first_bias = noise(key_list[8], (C,), 0.5, 3.0, (), jnp.float32)
    second_gain = jnp.clip(1.0 + 0.18 * jax.random.normal(key_list[9], (C,), jnp.float32), 0.1, 1.9)
    second_weight = noise(key_list[10], (3, 3, 3 * C, C), (27 * C) ** -0.5, 0.0625)
    second_bias = noise(key_list[11], (C,), 0.5, 3.0, (), jnp.float32)
    return dict(latent=latent, routing=routing, counts=counts, offsets=offsets, in_weight=in_weight, in_bias=in_bias, first_gain=first_gain, first_weight=first_weight, first_bias=first_bias, second_gain=second_gain, second_weight=second_weight, second_bias=second_bias)


def convolve(source, weight, bias_vec):
    frames = source.shape[0] - 2
    row_count = source.shape[1] - 2
    col_count = source.shape[2]
    padded = jnp.pad(source, ((0, 0), (0, 0), (1, 1), (0, 0)))
    summed = jnp.zeros((frames, row_count, col_count, weight.shape[-1]), jnp.float32)
    for step_t in range(3):
        for step_y in range(3):
            window = padded[step_t:step_t + frames, step_y:step_y + row_count]
            stacked = jnp.concatenate([window[:, :, step_x:step_x + col_count] for step_x in range(3)], axis=-1)
            summed = summed + jnp.einsum('abcd,de->abce', stacked.astype(jnp.float32), weight[step_t, step_y].astype(jnp.float32))
    return summed + bias_vec

def norm_silu(values, gain_vec):
    values = values.astype(jnp.float32)
    scaled = values * lax.rsqrt(lax.optimization_barrier(jnp.mean(values * values, axis=-1, keepdims=True)) + 1e-06)
    return jax.nn.silu(scaled * gain_vec).astype(jnp.bfloat16)

def pad_edges(frames_block):
    return jnp.pad(frames_block, ((2, 0), (1, 1), (0, 0), (0, 0)))

def reference(latent, routing, counts, offsets, in_weight, in_bias, first_gain, first_weight, first_bias, second_gain, second_weight, second_bias):
    frame_total = SPANS * FR
    span_of = jnp.arange(frame_total, dtype=jnp.int32) // FR

    def decode(video_index):
        frames_in = latent[:, :, video_index].reshape(frame_total, WROWS, COLS, Z)
        live_mask = ((span_of >= offsets[video_index]) & (span_of < offsets[video_index] + counts[video_index])).astype(jnp.float32)[:, None, None, None]
        latent_frames = (frames_in * live_mask).astype(jnp.bfloat16)
        hidden = (convolve(pad_edges(latent_frames), in_weight, in_bias) * live_mask).astype(jnp.bfloat16)
        middle = convolve(pad_edges(norm_silu(hidden, first_gain)), first_weight, first_bias) * live_mask
        result = convolve(pad_edges(norm_silu(middle, second_gain)), second_weight, second_bias)
        return ((result + hidden.astype(jnp.float32)) * live_mask).astype(jnp.bfloat16)
    decoded = lax.map(decode, jnp.arange(VIDS, dtype=jnp.int32))
    placed = jnp.zeros_like(decoded).at[routing].set(decoded)
    group_count = VIDS // VPG
    placed = placed.reshape(group_count, VPG, SPANS, FR, BANDS, ROWS, COLS, C)
    placed = jnp.transpose(placed, (2, 3, 0, 4, 1, 5, 6, 7)).reshape(SPANS, FR, VIDS * WROWS, COLS, C)
    return jnp.roll(placed, -(BANDS // 2) * VPG * ROWS, axis=2)
```

```python
import jax
import jax.numpy as jnp
import ml_dtypes
import numpy as np
from jax import lax
from jax.experimental import pallas as pl
from jax.experimental.pallas import tpu as pltpu
from jax.sharding import PartitionSpec as P

BANDS = 4
VPG = 2
F32 = jnp.float32
BF16 = jnp.bfloat16
VMEM_LIMIT = 60 << 20


def from_behind(value, axis, by):
    devices = lax.axis_size(axis)
    return lax.ppermute(value, axis, [(i, i + by) for i in range(devices - by)])


def neighbour_bands(value, axis, down):
    count = lax.axis_size(axis)
    pairs = []
    for device in range(count):
        band = ((device + BANDS // 2) % count) % BANDS
        if down and band < BANDS - 1:
            pairs.append((device, (device + 1) % count))
        if not down and band > 0:
            pairs.append((device, (device - 1) % count))
    return lax.ppermute(value, axis, pairs)


def act(values, gain):
    scale = lax.rsqrt(jnp.mean(values * values, axis=-1, keepdims=True) + 1e-06)
    half = values * scale * (0.5 * gain)
    return half * (1.0 + jnp.tanh(half))


def column_parts(even, odd):
    rows = even.shape[0]
    pair = lax.broadcasted_iota(jnp.int32, (rows, 1), 0) % 64
    odd_before = jnp.where(pair == 0, 0.0, pltpu.roll(odd, 1, 0))
    even_after = jnp.where(pair == 63, 0.0, pltpu.roll(even, rows - 1, 0))
    return odd_before - odd, even + odd, odd - even, even - even_after


def route_kernel(routing_ref, far_ref, near_ref, own_ref, sent_ref):
    rows = sent_ref.shape[0]
    lanes = own_ref.shape[0]
    slot_count = routing_ref.shape[0]
    lane = lax.broadcasted_iota(jnp.int32, (1, lanes), 1)
    slot_of_lane = jnp.full((1, lanes), -1, jnp.int32)
    for v in range(slot_count):
        slot_of_lane = jnp.where(lane // 4 == v, routing_ref[v], slot_of_lane)
    row = lax.broadcasted_iota(jnp.int32, (rows, 1), 0)
    placed = (row // 8 + BANDS // 2) % (rows // 8)
    slot_of_row = (placed // BANDS) * VPG + (row // 4) % VPG
    pick = (slot_of_row == slot_of_lane) & (row % 4 == lane % 4)
    pick = jnp.where(pick, 1.0, 0.0).astype(BF16)
    sent_ref[...] = jnp.zeros(sent_ref.shape, BF16)
    for s, ref in enumerate((far_ref, near_ref, own_ref)):
        moved = jnp.dot(pick, ref[...], preferred_element_type=F32)
        for pair in range(rows // 16):
            parts = []
            for device in (2 * pair, 2 * pair + 1):
                start = ((device + BANDS // 2) % BANDS) * 144
                parts.append(moved[device * 8 : device * 8 + 8, start : start + 336])
            block = jnp.concatenate(parts, axis=0).astype(BF16)
            sent_ref[pair * 16 : pair * 16 + 16, s * 384 : s * 384 + 336] = block


def weight_kernel(taps_ref, out_ref):
    depth = out_ref.shape[2]
    g0, g1, g2 = (taps_ref[0, k * depth : (k + 1) * depth, :] for k in range(3))
    ends = 0.5 * (g0.astype(F32) + g2.astype(F32))
    middle = 0.5 * g1.astype(F32)
    out_ref[0, 0] = g0
    out_ref[1, 0] = (ends + middle).astype(BF16)
    out_ref[2, 0] = (ends - middle).astype(BF16)
    out_ref[3, 0] = g2


def column_weights(weight):
    a, b, depth, channels = weight.shape
    taps = weight.reshape(a * b, depth, channels)
    shape = (4, a * b, depth // 3, channels)
    return pl.pallas_call(
        weight_kernel,
        grid=(a * b,),
        in_specs=[pl.BlockSpec((1, depth, channels), lambda t: (t, 0, 0))],
        out_specs=pl.BlockSpec((4, 1, depth // 3, channels), lambda t: (0, t, 0, 0)),
        out_shape=jax.ShapeDtypeStruct(shape, BF16),
        compiler_params=pltpu.CompilerParams(vmem_limit_bytes=16 << 20),
        cost_estimate=pl.CostEstimate(
            flops=0, bytes_accessed=2 * weight.size + 8 * weight.size // 3, transcendentals=0
        ),
        name="column_weights",
    )(taps)


def video_spans(place_ref, routing_ref, counts_ref, offsets_ref):
    found = []
    for p in range(VPG):
        slot = (place_ref[0] // BANDS) * VPG + p
        first = jnp.int32(0)
        end = jnp.int32(0)
        for v in range(routing_ref.shape[0]):
            here = routing_ref[v] == slot
            first = jnp.where(here, offsets_ref[v], first)
            end = jnp.where(here, offsets_ref[v] + counts_ref[v], end)
        found.append((first, end))
    return found


def live_mask(spans, span, inside, rows):
    flags = [
        jnp.where((span >= first) & (span < end) & inside, 1.0, 0.0) for first, end in spans
    ]
    row = lax.broadcasted_iota(jnp.int32, (rows, 1), 0)
    return jnp.where(row < rows // 2, flags[0], flags[1])


def input_kernel(
    place_ref,
    routing_ref,
    counts_ref,
    offsets_ref,
    planes_ref,
    weight_ref,
    bias_ref,
    gain_ref,
    parts_ref,
    hidden_ref,
):
    row = pl.program_id(0)
    frames = parts_ref.shape[2] // 128
    bias = bias_ref[...]
    gain = gain_ref[...]
    spans = video_spans(place_ref, routing_ref, counts_ref, offsets_ref)
    window_row = (place_ref[0] % BANDS) * 3 - 1 + row
    inside = (window_row >= 0) & (window_row < 3 * BANDS)
    for f in range(frames):
        taps = []
        for a in range(3):
            for b in range(3):
                s, k = divmod(f + a, 3)
                start = pl.multiple_of(s * 384 + k * 16 + (row + b) * 48, 16)
                tap = planes_ref[pl.ds(start, 16), :]
                taps += [tap[:, p * 128 : (p + 1) * 128] for p in range(4)]
        patch = jnp.concatenate(taps, axis=0)
        both = lax.dot_general(
            patch, weight_ref[...], (((0,), (0,)), ((), ())), preferred_element_type=F32
        )
        span = place_ref[1] + (f + 2) // 3 - 2
        mask = live_mask(spans, span, inside, 128)
        sides = []
        for side in range(2):
            values = both[:, side * 384 : (side + 1) * 384] + bias
            hidden = (values * mask).astype(BF16)
            if f >= frames - 3:

                @pl.when(row < 4)
                def _(hidden=hidden, f=f, side=side):
                    hidden_ref[0, f - (frames - 3), side] = hidden

            sides.append(act(hidden.astype(F32), gain))
        for i, part in enumerate(column_parts(*sides)):
            parts_ref[i, 0, f * 128 : (f + 1) * 128, :] = part.astype(BF16)


def products(load, weight_ref, rows, size):
    total = None
    for b in range(3):
        for a in range(3):
            term = jnp.dot(
                load(rows + b, a * 128, size), weight_ref[0, 3 * a + b], preferred_element_type=F32
            )
            total = term if total is None else total + term
    return total


def first_kernel(
    place_ref,
    routing_ref,
    counts_ref,
    offsets_ref,
    parts_ref,
    weight_ref,
    bias_ref,
    gain_ref,
    top_ref,
    bottom_ref,
    second_ref,
    terms_ref,
):
    step = pl.program_id(0)
    out_rows = terms_ref.shape[1]
    size = terms_ref.shape[2]
    for row in range(out_rows):
        terms_ref[step, row] = products(
            lambda r, start, n: parts_ref[0, r, start : start + n, :], weight_ref, row, size
        )

    @pl.when(step == 3)
    def _():
        bias = bias_ref[...]
        gain = gain_ref[...]
        spans = video_spans(place_ref, routing_ref, counts_ref, offsets_ref)
        for row in range(out_rows):

            def one_frame(f, carry):
                at = pl.ds(pl.multiple_of(f * 128, 128), 128)
                span = place_ref[1] + (f + 1) // 3 - 1
                mask = live_mask(spans, span, True, 128)
                mixed = terms_ref[1, row, at], terms_ref[2, row, at]
                even = terms_ref[0, row, at] + mixed[0] + mixed[1]
                odd = mixed[0] - mixed[1] - terms_ref[3, row, at]
                even = act((even + bias) * mask, gain)
                odd = act((odd + bias) * mask, gain)
                for edge_row, ref in ((0, top_ref), (out_rows - 1, bottom_ref)):
                    if row == edge_row:
                        ref[f, 0] = even.astype(BF16)
                        ref[f, 1] = odd.astype(BF16)
                for i, part in enumerate(column_parts(even, odd)):
                    second_ref[i, row, at, :] = part.astype(BF16)
                return carry

            lax.fori_loop(0, size // 128, one_frame, 0)


def second_kernel(
    place_ref,
    routing_ref,
    counts_ref,
    offsets_ref,
    parts_ref,
    above_ref,
    below_ref,
    weight_ref,
    bias_ref,
    hidden_ref,
    out_ref,
    halo_ref,
    terms_ref,
    line_ref,
):
    step = pl.program_id(0)
    out_rows = terms_ref.shape[1]
    size = terms_ref.shape[2]

    @pl.when(step == 0)
    def _():
        def one_frame(f, carry):
            at = pl.ds(pl.multiple_of(f * 128, 128), 128)
            for side, ref in enumerate((above_ref, below_ref)):
                even, odd = ref[f, 0].astype(F32), ref[f, 1].astype(F32)
                for i, part in enumerate(column_parts(even, odd)):
                    halo_ref[i, side, at, :] = part.astype(BF16)
            return carry

        lax.fori_loop(0, halo_ref.shape[2] // 128, one_frame, 0)

    def load(row, start, n):
        if row == 0:
            return halo_ref[step, 0, start : start + n, :]
        if row == out_rows + 1:
            return halo_ref[step, 1, start : start + n, :]
        return parts_ref[0, row - 1, start : start + n, :]

    for row in range(out_rows):
        terms_ref[step, row] = products(load, weight_ref, row, size)

    @pl.when(step == 3)
    def _():
        bias = bias_ref[...]
        spans = video_spans(place_ref, routing_ref, counts_ref, offsets_ref)
        lives = [
            jnp.where((place_ref[1] >= first) & (place_ref[1] < end), 1.0, 0.0)
            for first, end in spans
        ]
        for row in range(out_rows):

            def one_frame(f, carry):
                for video in range(2):
                    at = pl.ds(pl.multiple_of(f * 128 + video * 64, 64), 64)
                    mixed = terms_ref[1, row, at], terms_ref[2, row, at]
                    even = terms_ref[0, row, at] + mixed[0] + mixed[1]
                    odd = mixed[0] - mixed[1] - terms_ref[3, row, at]
                    here = slice(video * 64, video * 64 + 64)
                    live = lives[video]
                    even = (even + bias + hidden_ref[row, f, 0, here].astype(F32)) * live
                    odd = (odd + bias + hidden_ref[row, f, 1, here].astype(F32)) * live
                    for lane in range(3):
                        cut = slice(lane * 128, lane * 128 + 128)
                        line_ref[lane, pl.ds(0, 64, stride=2), :] = even[:, cut]
                        line_ref[lane, pl.ds(1, 64, stride=2), :] = odd[:, cut]
                    for lane in range(3):
                        cut = slice(lane * 128, lane * 128 + 128)
                        out_ref[f, video * out_rows + row, :, cut] = line_ref[lane].astype(BF16)
                return carry

            lax.fori_loop(0, size // 128, one_frame, 0)


def whole(shape):
    return pl.BlockSpec(shape, lambda *_: (0,) * len(shape))


def by_step(shape):
    return pl.BlockSpec(shape, lambda i: (i,) + (0,) * (len(shape) - 1))


SMEM = pl.BlockSpec(memory_space=pltpu.SMEM)
VMEM = pl.BlockSpec(memory_space=pltpu.VMEM)


def params():
    return pltpu.CompilerParams(vmem_limit_bytes=VMEM_LIMIT)


def on_device(
    latent,
    routing,
    counts,
    offsets,
    in_weight,
    in_bias,
    first_gain,
    first_weight,
    first_bias,
    second_gain,
    second_weight,
    second_bias,
):
    groups = lax.axis_size("video")
    spans = lax.axis_size("tm")
    _, span_frames, videos, window_rows, local_cols, zdim = latent.shape
    row_count = window_rows // BANDS
    channels = in_weight.shape[-1]
    pairs = groups * local_cols // 2
    span_index = lax.axis_index("tm")
    device_index = lax.axis_index("video")

    live = (span_index >= offsets) & (span_index < offsets + counts)
    own = jnp.transpose(latent[0], (1, 3, 2, 0, 4)) * live[:, None, None, None, None].astype(BF16)
    own = jnp.pad(own, ((0, 0), (0, 0), (2, 2), (0, 0), (0, 0)))
    own = own.reshape(videos * local_cols, (window_rows + 4) * span_frames * zdim)
    near, far = from_behind(own, "tm", 1), from_behind(own, "tm", 2)
    frames = 3 * span_frames
    sent = pl.pallas_call(
        route_kernel,
        in_specs=[SMEM] + [VMEM] * 3,
        out_specs=VMEM,
        out_shape=jax.ShapeDtypeStruct((groups * VPG * local_cols, 3 * 384), BF16),
        compiler_params=pltpu.CompilerParams(vmem_limit_bytes=16 << 20),
        name="route",
    )(routing, far, near, own)
    sent = sent.reshape(groups, VPG * local_cols, 3 * 384)
    got = lax.all_to_all(sent, "video", 0, 0, tiled=True)

    source = np.arange(groups * VPG * local_cols)
    source_col = (source // (VPG * local_cols)) * local_cols + source % local_cols
    source_video = (source // local_cols) % VPG
    pair = np.arange(pairs)
    wanted = np.stack([2 * pair - 1, 2 * pair, 2 * pair + 1, 2 * pair + 2])
    lanes = (source_col[:, None, None, None] == wanted[:, None, :]) & (
        source_video[:, None, None, None] == np.arange(VPG)[:, None]
    )
    lanes = lanes.reshape(source.size, 4 * VPG * pairs).astype(ml_dtypes.bfloat16)
    planes = lax.dot_general(
        got.reshape(source.size, 3 * 384),
        lanes,
        (((0,), (0,)), ((), ())),
        preferred_element_type=F32,
    ).astype(BF16)
    my_placed = (device_index + BANDS // 2) % groups
    place = jnp.stack([my_placed, span_index])
    scalars = (place, routing, counts, offsets)

    in_frames, mid_frames = frames - 2, frames - 4
    width = VPG * pairs
    rows5_n = row_count + 2

    zero = jnp.zeros(in_weight.shape[:2] + (zdim, channels), BF16)
    in_taps = jnp.concatenate(
        [
            jnp.concatenate([in_weight, zero], axis=2),
            jnp.concatenate([zero, in_weight], axis=2),
        ],
        axis=3,
    ).reshape(-1, 2 * channels)

    first_parts, hidden = pl.pallas_call(
        input_kernel,
        grid=(rows5_n,),
        in_specs=[
            *[SMEM] * 4,
            whole(planes.shape),
            whole(in_taps.shape),
            whole((channels,)),
            whole((channels,)),
        ],
        out_specs=[
            pl.BlockSpec((4, 1, in_frames * width, channels), lambda r: (0, r, 0, 0)),
            pl.BlockSpec(
                (1, span_frames, 2, width, channels),
                lambda r: (jnp.clip(r - 1, 0, row_count - 1), 0, 0, 0, 0),
            ),
        ],
        out_shape=[
            jax.ShapeDtypeStruct((4, rows5_n, in_frames * width, channels), BF16),
            jax.ShapeDtypeStruct((row_count, span_frames, 2, width, channels), BF16),
        ],
        compiler_params=params(),
        name="input_conv",
    )(*scalars, planes, in_taps, in_bias, first_gain)

    top, bottom, second_parts = pl.pallas_call(
        first_kernel,
        grid=(4,),
        in_specs=[
            *[SMEM] * 4,
            by_step((1, rows5_n, in_frames * width, channels)),
            by_step((1, 9, channels, channels)),
            whole((channels,)),
            whole((channels,)),
        ],
        out_specs=[
            whole((mid_frames, 2, width, channels)),
            whole((mid_frames, 2, width, channels)),
            whole((4, row_count, mid_frames * width, channels)),
        ],
        out_shape=[
            jax.ShapeDtypeStruct((mid_frames, 2, width, channels), BF16),
            jax.ShapeDtypeStruct((mid_frames, 2, width, channels), BF16),
            jax.ShapeDtypeStruct((4, row_count, mid_frames * width, channels), BF16),
        ],
        scratch_shapes=[pltpu.VMEM((4, row_count, mid_frames * width, channels), F32)],
        compiler_params=params(),
        name="first_conv",
    )(*scalars, first_parts, column_weights(first_weight), first_bias, second_gain)

    above = neighbour_bands(bottom, "video", True)
    below = neighbour_bands(top, "video", False)

    out = pl.pallas_call(
        second_kernel,
        grid=(4,),
        in_specs=[
            *[SMEM] * 4,
            by_step((1, row_count, mid_frames * width, channels)),
            whole(above.shape),
            whole(below.shape),
            by_step((1, 9, channels, channels)),
            whole((channels,)),
            pl.BlockSpec((row_count, span_frames, 2, width, channels), lambda i: (0, 0, 0, 0, 0)),
        ],
        out_specs=whole((span_frames, VPG * row_count, 2 * pairs, channels)),
        out_shape=jax.ShapeDtypeStruct((span_frames, VPG * row_count, 2 * pairs, channels), BF16),
        scratch_shapes=[
            pltpu.VMEM((4, 2, mid_frames * width, channels), BF16),
            pltpu.VMEM((4, row_count, span_frames * width, channels), F32),
            pltpu.VMEM((3, 2 * pairs, 128), F32),
        ],
        compiler_params=params(),
        name="second_conv",
    )(
        *scalars,
        second_parts,
        above,
        below,
        column_weights(second_weight),
        second_bias,
        hidden,
    )
    return out[None]


def solution(mesh):
    in_specs = (P("tm", None, None, None, "video", None),) + (P(),) * 11
    out_specs = P("tm", None, "video", None, None)
    return jax.shard_map(
        on_device, mesh=mesh, in_specs=in_specs, out_specs=out_specs, check_vma=False
    )
```

```python
import jax
import jax.numpy as jnp
import ml_dtypes
import numpy as np
from jax import lax
from jax.experimental import pallas as pl
from jax.experimental.pallas import tpu as pltpu
from jax.sharding import PartitionSpec as P

BANDS = 4
VPG = 2
F32 = jnp.float32
BF16 = jnp.bfloat16
VMEM_LIMIT = 60 << 20


def neighbour_bands(value, axis, down):
    count = lax.axis_size(axis)
    pairs = []
    for device in range(count):
        band = ((device + BANDS // 2) % count) % BANDS
        if down and band < BANDS - 1:
            pairs.append((device, (device + 1) % count))
        if not down and band > 0:
            pairs.append((device, (device - 1) % count))
    return lax.ppermute(value, axis, pairs)


def act(values, gain):
    scale = lax.rsqrt(jnp.mean(values * values, axis=-1, keepdims=True) + 1e-06)
    half = values * scale * (0.5 * gain)
    return half * (1.0 + jnp.tanh(half))


def column_parts(even, odd):
    rows = even.shape[0]
    pair = lax.broadcasted_iota(jnp.int32, (rows, 1), 0) % 64
    odd_before = jnp.where(pair == 0, 0.0, pltpu.roll(odd, 1, 0))
    even_after = jnp.where(pair == 63, 0.0, pltpu.roll(even, rows - 1, 0))
    return odd_before - odd, even + odd, odd - even, even - even_after


def route_kernel(place_ref, routing_ref, counts_ref, offsets_ref, own_ref, sent_ref):
    span_count, rows = sent_ref.shape[:2]
    lanes = own_ref.shape[0]
    span = place_ref[1]
    lane = lax.broadcasted_iota(jnp.int32, (1, lanes), 1)
    slot_of_lane = jnp.full((1, lanes), -1, jnp.int32)
    for v in range(routing_ref.shape[0]):
        live = (span >= offsets_ref[v]) & (span < offsets_ref[v] + counts_ref[v])
        slot = jnp.where(live, routing_ref[v], -1)
        slot_of_lane = jnp.where(lane // 4 == v, slot, slot_of_lane)
    row = lax.broadcasted_iota(jnp.int32, (rows, 1), 0)
    placed = (row // 8 + BANDS // 2) % (rows // 8)
    slot_of_row = (placed // BANDS) * VPG + (row // 4) % VPG
    pick = (slot_of_row == slot_of_lane) & (row % 4 == lane % 4)
    pick = jnp.where(pick, 1.0, 0.0).astype(BF16)
    moved = jnp.dot(pick, own_ref[...], preferred_element_type=F32)
    edge = jnp.zeros((rows, 96), F32)
    moved = jnp.concatenate([edge, moved, edge], axis=1)
    tail = jnp.zeros((8, 48), F32)
    reach = [jnp.where((k >= span) & (k <= span + 2), 1.0, 0.0) for k in range(span_count)]
    for pair in range(rows // 16):
        parts = []
        for device in (2 * pair, 2 * pair + 1):
            start = ((device + BANDS // 2) % BANDS) * 144
            window = moved[device * 8 : device * 8 + 8, start : start + 336]
            parts.append(jnp.concatenate([window, tail], axis=1))
        block = jnp.concatenate(parts, axis=0)
        for k in range(span_count):
            sent_ref[k, pair * 16 : pair * 16 + 16, :] = (block * reach[k]).astype(BF16)


def weight_copies(weight_ref, taps_ref, middle_ref, sems, which):
    depth = middle_ref.shape[0] // 3
    target = {0: taps_ref.at[0], 1: middle_ref, 2: taps_ref.at[3]}[which]
    return [
        pltpu.make_async_copy(
            weight_ref.at[3 * a + b, which * depth : (which + 1) * depth, :],
            target.at[a * depth : (a + 1) * depth, b * depth : (b + 1) * depth],
            sems.at[which, 3 * a + b],
        )
        for a in range(3)
        for b in range(3)
    ]


def mix_weights(taps_ref, middle_ref):
    size = 128

    def one_part(t, carry):
        at = pl.ds(pl.multiple_of(t * size, size), size)
        ends = 0.5 * (taps_ref[0, at].astype(F32) + taps_ref[3, at].astype(F32))
        middle = 0.5 * middle_ref[at].astype(F32)
        taps_ref[1, at] = (ends + middle).astype(BF16)
        taps_ref[2, at] = (ends - middle).astype(BF16)
        return carry

    lax.fori_loop(0, middle_ref.shape[0] // size, one_part, 0)


def video_spans(place_ref, routing_ref, counts_ref, offsets_ref):
    found = []
    for p in range(VPG):
        slot = (place_ref[0] // BANDS) * VPG + p
        first = jnp.int32(0)
        end = jnp.int32(0)
        for v in range(routing_ref.shape[0]):
            here = routing_ref[v] == slot
            first = jnp.where(here, offsets_ref[v], first)
            end = jnp.where(here, offsets_ref[v] + counts_ref[v], end)
        found.append((first, end))
    return found


def live_mask(spans, span, inside, rows):
    flags = [
        jnp.where((span >= first) & (span < end) & inside, 1.0, 0.0) for first, end in spans
    ]
    row = lax.broadcasted_iota(jnp.int32, (rows, 1), 0)
    return jnp.where(row < rows // 2, flags[0], flags[1])


def add_products(terms_ref, step, row, written, load, taps_ref):
    out_rows, size, channels = terms_ref.shape[1:]
    taps = [b for b in range(3) if 0 <= row - b < out_rows]
    first, last = taps[0], taps[-1] + 1
    stacked = jnp.concatenate([load(a * 128, size) for a in range(3)], axis=1)
    both = jnp.dot(
        stacked,
        taps_ref[step, :, first * channels : last * channels],
        preferred_element_type=F32,
    )
    for b in taps:
        term = both[:, (b - first) * channels : (b - first + 1) * channels]
        if row - b in written:
            terms_ref[step, row - b] += term
        else:
            terms_ref[step, row - b] = term
        written.add(row - b)


def first_kernel(
    place_ref,
    routing_ref,
    counts_ref,
    offsets_ref,
    got_ref,
    lanes_ref,
    in_taps_ref,
    in_bias_ref,
    first_gain_ref,
    weight_ref,
    bias_ref,
    gain_ref,
    hidden_ref,
    top_ref,
    bottom_ref,
    second_ref,
    planes_ref,
    parts_ref,
    taps_ref,
    middle_ref,
    terms_ref,
    sems,
):
    copies = [weight_copies(weight_ref, taps_ref, middle_ref, sems, k) for k in range(3)]
    for column in copies:
        for copy in column:
            copy.start()
    spans = video_spans(place_ref, routing_ref, counts_ref, offsets_ref)
    span_count = got_ref.shape[0]
    for k in range(span_count):
        planes_ref[k * 384 : (k + 1) * 384, :] = lax.dot_general(
            got_ref[k], lanes_ref[...], (((0,), (0,)), ((), ())), preferred_element_type=F32
        ).astype(BF16)
    in_bias = in_bias_ref[...]
    first_gain = first_gain_ref[...]
    in_rows = parts_ref.shape[1]
    frames = parts_ref.shape[2] // 128
    out_rows, size = terms_ref.shape[1:3]

    def input_row(row, carry):
        window_row = (place_ref[0] % BANDS) * out_rows - 1 + row
        inside = (window_row >= 0) & (window_row < out_rows * BANDS)
        own = jnp.clip(row - 1, 0, out_rows - 1)
        for f in range(frames):
            taps = []
            for a in range(3):
                s, k = divmod(f + a, 3)
                base = ((place_ref[1] + span_count - 2 + s) % span_count) * 384
                for b in range(3):
                    start = pl.multiple_of(base + k * 16 + (row + b) * 48, 16)
                    tap = planes_ref[pl.ds(start, 16), :]
                    taps += [tap[:, p * 128 : (p + 1) * 128] for p in range(4)]
            patch = jnp.concatenate(taps, axis=0)
            both = lax.dot_general(
                patch, in_taps_ref[...], (((0,), (0,)), ((), ())), preferred_element_type=F32
            )
            span = place_ref[1] + (f + 2) // 3 - 2
            mask = live_mask(spans, span, inside, 128)
            sides = []
            for side in range(2):
                values = both[:, side * 384 : (side + 1) * 384] + in_bias
                hidden = (values * mask).astype(BF16)
                if f >= frames - 3:

                    @pl.when(row <= out_rows)
                    def _(hidden=hidden, f=f, side=side):
                        hidden_ref[own, f - (frames - 3), side] = hidden

                sides.append(act(hidden.astype(F32), first_gain))
            for i, part in enumerate(column_parts(*sides)):
                parts_ref[i, row, f * 128 : (f + 1) * 128, :] = part.astype(BF16)
        return carry

    lax.fori_loop(0, in_rows, input_row, 0)

    for column in copies:
        for copy in column:
            copy.wait()
    mix_weights(taps_ref, middle_ref)

    def one_step(step, carry):
        written = set()
        for row in range(in_rows):
            add_products(
                terms_ref,
                step,
                row,
                written,
                lambda start, n, row=row: parts_ref[step, row, start : start + n, :],
                taps_ref,
            )
        return carry

    lax.fori_loop(0, 4, one_step, 0)

    bias = bias_ref[...]
    gain = gain_ref[...]
    for row in range(out_rows):

        def one_frame(f, carry, row=row):
            at = pl.ds(pl.multiple_of(f * 128, 128), 128)
            span = place_ref[1] + (f + 1) // 3 - 1
            mask = live_mask(spans, span, True, 128)
            mixed = terms_ref[1, row, at], terms_ref[2, row, at]
            even = terms_ref[0, row, at] + mixed[0] + mixed[1]
            odd = mixed[0] - mixed[1] - terms_ref[3, row, at]
            even = act((even + bias) * mask, gain)
            odd = act((odd + bias) * mask, gain)
            for edge_row, ref in ((0, top_ref), (out_rows - 1, bottom_ref)):
                if row == edge_row:
                    ref[f, 0] = even.astype(BF16)
                    ref[f, 1] = odd.astype(BF16)
            for i, part in enumerate(column_parts(even, odd)):
                second_ref[i, row, at, :] = part.astype(BF16)
            return carry

        lax.fori_loop(0, size // 128, one_frame, 0)


def write_line(line_ref, even, odd):
    for lane in range(3):
        cut = slice(lane * 128, lane * 128 + 128)
        line_ref[lane, pl.ds(0, 64, stride=2), :] = even[:, cut]
        line_ref[lane, pl.ds(1, 64, stride=2), :] = odd[:, cut]
    return jnp.concatenate([line_ref[lane] for lane in range(3)], axis=1).astype(BF16)


def video_lives(place_ref, routing_ref, counts_ref, offsets_ref):
    spans = video_spans(place_ref, routing_ref, counts_ref, offsets_ref)
    return [
        jnp.where((place_ref[1] >= first) & (place_ref[1] < end), 1.0, 0.0) for first, end in spans
    ]


def inner_kernel(
    place_ref,
    routing_ref,
    counts_ref,
    offsets_ref,
    second_ref,
    weight_ref,
    bias_ref,
    hidden_ref,
    out_ref,
    sums_ref,
    edge_taps_ref,
    parts_ref,
    taps_ref,
    middle_ref,
    terms_ref,
    line_ref,
    sems,
    part_sems,
    edge_sems,
):
    out_rows, size, channels = terms_ref.shape[1:]
    copies = [weight_copies(weight_ref, taps_ref, middle_ref, sems, k) for k in range(3)]
    parts = [
        pltpu.make_async_copy(second_ref.at[i], parts_ref.at[i], part_sems.at[i])
        for i in range(4)
    ]
    for k, i in ((0, 0), (2, 3), (1, 1)):
        parts[i].start()
        for copy in copies[k]:
            copy.start()
    parts[2].start()

    def one_step(step):
        written = set()
        for row in range(1, out_rows + 1):
            add_products(
                terms_ref,
                step,
                row,
                written,
                lambda start, n, row=row: parts_ref[step, row - 1, start : start + n, :],
                taps_ref,
            )

    for k, i in ((0, 0), (2, 3)):
        parts[i].wait()
        for copy in copies[k]:
            copy.wait()

    def end_steps(n, carry):
        one_step(n * 3)
        return carry

    def middle_steps(n, carry):
        one_step(n + 1)
        return carry

    lax.fori_loop(0, 2, end_steps, 0)
    for copy in copies[1]:
        copy.wait()
    parts[1].wait()
    parts[2].wait()
    mix_weights(taps_ref, middle_ref)
    edge_copies = [
        pltpu.make_async_copy(
            taps_ref.at[:, :, 2 * side * channels : (2 * side + 1) * channels],
            edge_taps_ref.at[side],
            edge_sems.at[side],
        )
        for side in range(2)
    ]
    for copy in edge_copies:
        copy.start()
    lax.fori_loop(0, 2, middle_steps, 0)

    bias = bias_ref[...]
    lives = video_lives(place_ref, routing_ref, counts_ref, offsets_ref)
    for row in range(out_rows):
        side = {0: 0, out_rows - 1: 1}.get(row)

        def one_frame(f, carry, row=row, side=side):
            for video in range(2):
                at = pl.ds(pl.multiple_of(f * 128 + video * 64, 64), 64)
                here = slice(video * 64, video * 64 + 64)
                mixed = terms_ref[1, row, at], terms_ref[2, row, at]
                even = terms_ref[0, row, at] + mixed[0] + mixed[1]
                odd = mixed[0] - mixed[1] - terms_ref[3, row, at]
                even = (even + bias + hidden_ref[row, f, 0, here].astype(F32)) * lives[video]
                odd = (odd + bias + hidden_ref[row, f, 1, here].astype(F32)) * lives[video]
                if side is None:
                    out_ref[f, video * out_rows + row] = write_line(line_ref, even, odd)
                else:
                    sums_ref[side, 0, at] = even
                    sums_ref[side, 1, at] = odd
            return carry

        lax.fori_loop(0, size // 128, one_frame, 0)
    for copy in edge_copies:
        copy.wait()


def outer_kernel(
    place_ref,
    routing_ref,
    counts_ref,
    offsets_ref,
    inner_ref,
    above_ref,
    below_ref,
    taps_ref,
    sums_ref,
    out_ref,
    halo_ref,
    terms_ref,
    line_ref,
    ready_ref,
    sems,
):
    step = pl.program_id(0)
    size = terms_ref.shape[2]
    rows_per_video = out_ref.shape[1] // VPG

    @pl.when(step == 0)
    def _():
        def one_frame(f, carry):
            at = pl.ds(pl.multiple_of(f * 128, 128), 128)
            for side, ref in enumerate((above_ref, below_ref)):
                even, odd = ref[f, 0].astype(F32), ref[f, 1].astype(F32)
                for i, part in enumerate(column_parts(even, odd)):
                    halo_ref[i, side, at, :] = part.astype(BF16)
            return carry

        lax.fori_loop(0, halo_ref.shape[2] // 128, one_frame, 0)

    for side in range(2):
        stacked = jnp.concatenate(
            [halo_ref[step, side, a * 128 : a * 128 + size, :] for a in range(3)], axis=1
        )
        terms_ref[step, side] = jnp.dot(stacked, taps_ref[side, 0], preferred_element_type=F32)

    @pl.when(step == 3)
    def _():
        lives = video_lives(place_ref, routing_ref, counts_ref, offsets_ref)
        copies = []
        for f in range(size // 128):
            for side in range(2):
                for video in range(VPG):
                    at = slice(f * 128 + video * 64, f * 128 + video * 64 + 64)
                    mixed = terms_ref[1, side, at], terms_ref[2, side, at]
                    even = terms_ref[0, side, at] + mixed[0] + mixed[1]
                    odd = mixed[0] - mixed[1] - terms_ref[3, side, at]
                    even = sums_ref[side, 0, at] + even * lives[video]
                    odd = sums_ref[side, 1, at] + odd * lives[video]
                    n = len(copies)
                    ready_ref[n] = write_line(line_ref, even, odd)
                    row = video * rows_per_video + side * (rows_per_video - 1)
                    copies.append(
                        pltpu.make_async_copy(ready_ref.at[n], out_ref.at[f, row], sems.at[n])
                    )
                    copies[-1].start()
        for copy in copies:
            copy.wait()


def whole(shape):
    return pl.BlockSpec(shape, lambda *_: (0,) * len(shape))


SMEM = pl.BlockSpec(memory_space=pltpu.SMEM)
VMEM = pl.BlockSpec(memory_space=pltpu.VMEM)
ANY = pl.BlockSpec(memory_space=pl.ANY)


def params():
    return pltpu.CompilerParams(vmem_limit_bytes=VMEM_LIMIT)


def on_device(
    latent,
    routing,
    counts,
    offsets,
    in_weight,
    in_bias,
    first_gain,
    first_weight,
    first_bias,
    second_gain,
    second_weight,
    second_bias,
):
    groups = lax.axis_size("video")
    spans = lax.axis_size("tm")
    _, span_frames, videos, window_rows, local_cols, zdim = latent.shape
    row_count = window_rows // BANDS
    channels = in_weight.shape[-1]
    pairs = groups * local_cols // 2
    span_index = lax.axis_index("tm")
    device_index = lax.axis_index("video")

    my_placed = (device_index + BANDS // 2) % groups
    place = jnp.stack([my_placed, span_index])
    scalars = (place, routing, counts, offsets)

    own = jnp.transpose(latent[0], (1, 3, 2, 0, 4))
    own = own.reshape(videos * local_cols, window_rows * span_frames * zdim)
    chunk = VPG * local_cols
    sent = pl.pallas_call(
        route_kernel,
        in_specs=[SMEM] * 4 + [VMEM],
        out_specs=VMEM,
        out_shape=jax.ShapeDtypeStruct((spans, groups * chunk, 384), BF16),
        compiler_params=pltpu.CompilerParams(vmem_limit_bytes=16 << 20),
        name="route",
    )(*scalars, own)
    sent = sent.reshape(spans * groups, chunk, 384)
    got = lax.all_to_all(sent, ("tm", "video"), 0, 0, tiled=True)
    got = got.reshape(spans, groups * chunk, 384)

    source = np.arange(groups * VPG * local_cols)
    source_col = (source // (VPG * local_cols)) * local_cols + source % local_cols
    source_video = (source // local_cols) % VPG
    pair = np.arange(pairs)
    wanted = np.stack([2 * pair - 1, 2 * pair, 2 * pair + 1, 2 * pair + 2])
    lanes = (source_col[:, None, None, None] == wanted[:, None, :]) & (
        source_video[:, None, None, None] == np.arange(VPG)[:, None]
    )
    lanes = lanes.reshape(source.size, 4 * VPG * pairs).astype(ml_dtypes.bfloat16)
    frames = 3 * span_frames
    in_frames, mid_frames = frames - 2, frames - 4
    width = VPG * pairs
    rows5_n = row_count + 2

    zero = jnp.zeros(in_weight.shape[:2] + (zdim, channels), BF16)
    in_taps = jnp.concatenate(
        [
            jnp.concatenate([in_weight, zero], axis=2),
            jnp.concatenate([zero, in_weight], axis=2),
        ],
        axis=3,
    ).reshape(-1, 2 * channels)

    depth = 3 * channels
    raw_shape = (9, depth, channels)
    edge_shape = (mid_frames, 2, width, channels)
    part_shape = (4, row_count, mid_frames * width, channels)
    hidden_shape = (row_count, span_frames, 2, width, channels)
    hidden, top, bottom, second_parts = pl.pallas_call(
        first_kernel,
        in_specs=[SMEM] * 4 + [VMEM] * 5 + [ANY] + [VMEM] * 2,
        out_specs=[VMEM] * 4,
        out_shape=[
            jax.ShapeDtypeStruct(shape, BF16)
            for shape in (hidden_shape, edge_shape, edge_shape, part_shape)
        ],
        scratch_shapes=[
            pltpu.VMEM((spans * 384, 4 * width), BF16),
            pltpu.VMEM((4, rows5_n, in_frames * width, channels), BF16),
            pltpu.VMEM((4, depth, depth), BF16),
            pltpu.VMEM((depth, depth), BF16),
            pltpu.VMEM((4, row_count, mid_frames * width, channels), F32),
            pltpu.SemaphoreType.DMA((3, 9)),
        ],
        compiler_params=params(),
        name="first_conv",
    )(
        *scalars,
        got,
        lanes,
        in_taps,
        in_bias,
        first_gain,
        first_weight.reshape(raw_shape),
        first_bias,
        second_gain,
    )

    above = neighbour_bands(bottom, "video", True)
    below = neighbour_bands(top, "video", False)

    out_shape = (span_frames, VPG * row_count, 2 * pairs, channels)
    sums_shape = (2, 2, span_frames * width, channels)
    inner, sums, edge_taps = pl.pallas_call(
        inner_kernel,
        in_specs=[SMEM] * 4 + [ANY, ANY, VMEM, VMEM],
        out_specs=[VMEM, VMEM, ANY],
        out_shape=[
            jax.ShapeDtypeStruct(out_shape, BF16),
            jax.ShapeDtypeStruct(sums_shape, F32),
            jax.ShapeDtypeStruct((2, 4, depth, channels), BF16),
        ],
        scratch_shapes=[
            pltpu.VMEM(part_shape, BF16),
            pltpu.VMEM((4, depth, depth), BF16),
            pltpu.VMEM((depth, depth), BF16),
            pltpu.VMEM((4, row_count, span_frames * width, channels), F32),
            pltpu.VMEM((3, 2 * pairs, 128), F32),
            pltpu.SemaphoreType.DMA((3, 9)),
            pltpu.SemaphoreType.DMA((4,)),
            pltpu.SemaphoreType.DMA((2,)),
        ],
        compiler_params=params(),
        cost_estimate=pl.CostEstimate(
            flops=12 * 10**9, bytes_accessed=24 * 10**6, transcendentals=0
        ),
        name="second_conv_inner",
    )(*scalars, second_parts, second_weight.reshape(raw_shape), second_bias, hidden)

    out = pl.pallas_call(
        outer_kernel,
        grid=(4,),
        in_specs=[
            *[SMEM] * 4,
            ANY,
            whole(edge_shape),
            whole(edge_shape),
            pl.BlockSpec((2, 1, depth, channels), lambda i: (0, i, 0, 0)),
            whole(sums_shape),
        ],
        out_specs=ANY,
        out_shape=jax.ShapeDtypeStruct(out_shape, BF16),
        input_output_aliases={4: 0},
        scratch_shapes=[
            pltpu.VMEM((4, 2, mid_frames * width, channels), BF16),
            pltpu.VMEM((4, 2, span_frames * width, channels), F32),
            pltpu.VMEM((3, 2 * pairs, 128), F32),
            pltpu.VMEM((span_frames * 2 * VPG, 2 * pairs, channels), BF16),
            pltpu.SemaphoreType.DMA((span_frames * 2 * VPG,)),
        ],
        compiler_params=params(),
        name="second_conv_outer",
    )(*scalars, inner, above, below, edge_taps, sums)
    return out[None]


def solution(mesh):
    in_specs = (P("tm", None, None, None, "video", None),) + (P(),) * 11
    out_specs = P("tm", None, "video", None, None)
    return jax.shard_map(
        on_device, mesh=mesh, in_specs=in_specs, out_specs=out_specs, check_vma=False
    )
```

```python
import jax
import jax.numpy as jnp
import ml_dtypes
import numpy as np
from jax import lax
from jax.experimental import pallas as pl
from jax.experimental.pallas import tpu as pltpu
from jax.sharding import PartitionSpec as P

BANDS = 4
VPG = 2
F32 = jnp.float32
BF16 = jnp.bfloat16
VMEM_LIMIT = 60 << 20


def neighbour_bands(value, axis, down):
    count = lax.axis_size(axis)
    pairs = []
    for device in range(count):
        band = ((device + BANDS // 2) % count) % BANDS
        if down and band < BANDS - 1:
            pairs.append((device, (device + 1) % count))
        if not down and band > 0:
            pairs.append((device, (device - 1) % count))
    return lax.ppermute(value, axis, pairs)


def act(values, gain):
    scale = lax.rsqrt(jnp.mean(values * values, axis=-1, keepdims=True) + 1e-06)
    half = values * scale * (0.5 * gain)
    return half * (1.0 + jnp.tanh(half))


def column_parts(even, odd):
    return odd, even + odd, odd - even, even


def column_sums(terms):
    z0, z1, z2, z3 = terms
    rows = z0.shape[0]
    pair = lax.broadcasted_iota(jnp.int32, (rows, 1), 0) % 64
    before = jnp.where(pair == 0, 0.0, pltpu.roll(z0, 1, 0))
    after = jnp.where(pair == 63, 0.0, pltpu.roll(z3, rows - 1, 0))
    return before - z0 + (z1 + z2), after - z3 + (z1 - z2)


def route_kernel(place_ref, routing_ref, counts_ref, offsets_ref, own_ref, sent_ref):
    span_count, rows = sent_ref.shape[:2]
    lanes = own_ref.shape[0]
    span = place_ref[1]
    lane = lax.broadcasted_iota(jnp.int32, (1, lanes), 1)
    slot_of_lane = jnp.full((1, lanes), -1, jnp.int32)
    for v in range(routing_ref.shape[0]):
        live = (span >= offsets_ref[v]) & (span < offsets_ref[v] + counts_ref[v])
        slot = jnp.where(live, routing_ref[v], -1)
        slot_of_lane = jnp.where(lane // 4 == v, slot, slot_of_lane)
    row = lax.broadcasted_iota(jnp.int32, (rows, 1), 0)
    placed = (row // 8 + BANDS // 2) % (rows // 8)
    slot_of_row = (placed // BANDS) * VPG + (row // 4) % VPG
    pick = (slot_of_row == slot_of_lane) & (row % 4 == lane % 4)
    pick = jnp.where(pick, 1.0, 0.0).astype(BF16)
    moved = jnp.dot(pick, own_ref[...], preferred_element_type=F32)
    edge = jnp.zeros((rows, 96), F32)
    moved = jnp.concatenate([edge, moved, edge], axis=1)
    tail = jnp.zeros((8, 48), F32)
    reach = [jnp.where((k >= span) & (k <= span + 2), 1.0, 0.0) for k in range(span_count)]
    for pair in range(rows // 16):
        parts = []
        for device in (2 * pair, 2 * pair + 1):
            start = ((device + BANDS // 2) % BANDS) * 144
            window = moved[device * 8 : device * 8 + 8, start : start + 336]
            parts.append(jnp.concatenate([window, tail], axis=1))
        block = jnp.concatenate(parts, axis=0)
        for k in range(span_count):
            sent_ref[k, pair * 16 : pair * 16 + 16, :] = (block * reach[k]).astype(BF16)


def mix_kernel(weight_ref, out_ref, raw_ref, mixed_ref, sems, out_sems):
    taps = raw_ref.shape[0]
    depth = raw_ref.shape[1] // 3
    arriving = [
        pltpu.make_async_copy(weight_ref.at[t], raw_ref.at[t], sems.at[t]) for t in range(taps)
    ]
    for copy in arriving:
        copy.start()
    leaving = []
    for t in range(taps):
        arriving[t].wait()
        a, b = divmod(t, 3)
        lanes = slice(b * depth, (b + 1) * depth)

        def one_part(n, carry, t=t, a=a, lanes=lanes):
            g0, g1, g2 = (
                raw_ref[t, pl.ds(pl.multiple_of(k * depth + n * 64, 64), 64), :].astype(F32)
                for k in range(3)
            )
            ends = 0.5 * (g0 + g2)
            at = pl.ds(pl.multiple_of(a * depth + n * 64, 64), 64)
            mixed_ref[0, at, lanes] = (ends + 0.5 * g1).astype(BF16)
            mixed_ref[1, at, lanes] = (ends - 0.5 * g1).astype(BF16)
            return carry

        lax.fori_loop(0, depth // 64, one_part, 0)
        block = (slice(None), slice(a * depth, (a + 1) * depth), lanes)
        leaving.append(
            pltpu.make_async_copy(mixed_ref.at[block], out_ref.at[block], out_sems.at[t])
        )
        leaving[-1].start()
    for copy in leaving:
        copy.wait()


def mixed_weights(weight):
    taps, wide, channels = weight.shape
    depth = wide // 3
    shape = (2, 3 * depth, 3 * channels)
    return pl.pallas_call(
        mix_kernel,
        in_specs=[ANY],
        out_specs=ANY,
        out_shape=jax.ShapeDtypeStruct(shape, BF16),
        scratch_shapes=[
            pltpu.VMEM(weight.shape, BF16),
            pltpu.VMEM(shape, BF16),
            pltpu.SemaphoreType.DMA((taps,)),
            pltpu.SemaphoreType.DMA((taps,)),
        ],
        compiler_params=params(VMEM_LIMIT),
        cost_estimate=pl.CostEstimate(
            flops=0, bytes_accessed=2 * weight.size + 4 * weight.size // 3, transcendentals=0
        ),
        name="mixed_weights",
    )(weight)


def weight_copies(weight_ref, mixed_ref, taps_ref, sems, which, row_tap):
    depth = taps_ref.shape[1] // 3
    lanes = slice(row_tap * depth, (row_tap + 1) * depth)
    if which in (1, 2):
        return [
            pltpu.make_async_copy(
                mixed_ref.at[which - 1, :, lanes],
                taps_ref.at[which, :, lanes],
                sems.at[which, row_tap, 0],
            )
        ]
    column = 0 if which == 0 else 2
    return [
        pltpu.make_async_copy(
            weight_ref.at[3 * a + row_tap, column * depth : (column + 1) * depth, :],
            taps_ref.at[which, a * depth : (a + 1) * depth, lanes],
            sems.at[which, row_tap, a],
        )
        for a in range(3)
    ]


def video_spans(place_ref, routing_ref, counts_ref, offsets_ref):
    found = []
    for p in range(VPG):
        slot = (place_ref[0] // BANDS) * VPG + p
        first = jnp.int32(0)
        end = jnp.int32(0)
        for v in range(routing_ref.shape[0]):
            here = routing_ref[v] == slot
            first = jnp.where(here, offsets_ref[v], first)
            end = jnp.where(here, offsets_ref[v] + counts_ref[v], end)
        found.append((first, end))
    return found


def live_mask(spans, span, inside, rows):
    flags = [
        jnp.where((span >= first) & (span < end) & inside, 1.0, 0.0) for first, end in spans
    ]
    row = lax.broadcasted_iota(jnp.int32, (rows, 1), 0)
    return jnp.where(row < rows // 2, flags[0], flags[1])


def add_products(terms_refs, step, row, load, taps_ref, opening):
    size, channels = terms_refs[0].shape[1:]
    taps = [b for b in range(3) if 0 <= row - b < len(terms_refs)]
    first, last = taps[0], taps[-1] + 1
    stacked = jnp.concatenate([load(a * 128, size) for a in range(3)], axis=1)
    both = jnp.dot(
        stacked,
        taps_ref[step, :, first * channels : last * channels],
        preferred_element_type=F32,
    )
    for b in taps:
        term = both[:, (b - first) * channels : (b - first + 1) * channels]
        ref = terms_refs[row - b]
        if row - b in opening:
            ref[step] = term
        else:
            ref[step] += term


def first_kernel(
    place_ref,
    routing_ref,
    counts_ref,
    offsets_ref,
    got_ref,
    lanes_ref,
    in_taps_ref,
    in_bias_ref,
    first_gain_ref,
    weight_ref,
    mixed_ref,
    bias_ref,
    gain_ref,
    hidden_out_ref,
    row_0,
    row_1,
    row_2,
    planes_ref,
    taps_ref,
    hidden_ref,
    second_ref,
    parts_0,
    parts_1,
    parts_2,
    parts_3,
    parts_4,
    terms_0,
    terms_1,
    terms_2,
    sems,
    out_sems,
):
    parts_refs = (parts_0, parts_1, parts_2, parts_3, parts_4)
    terms_refs = (terms_0, terms_1, terms_2)
    in_rows, out_rows = len(parts_refs), len(terms_refs)
    frames = parts_0.shape[1] // 128
    out_frames = terms_0.shape[1] // 128
    copies = [
        [
            copy
            for which in range(4)
            for copy in weight_copies(weight_ref, mixed_ref, taps_ref, sems, which, b)
        ]
        for b in range(3)
    ]
    for column in copies:
        for copy in column:
            copy.start()
    spans = video_spans(place_ref, routing_ref, counts_ref, offsets_ref)
    span_count = got_ref.shape[0]
    for k in range(3):
        span = (place_ref[1] + span_count - 2 + k) % span_count
        planes_ref[k * 384 : (k + 1) * 384, :] = lax.dot_general(
            got_ref[span], lanes_ref[...], (((0,), (0,)), ((), ())), preferred_element_type=F32
        ).astype(BF16)
    in_bias = in_bias_ref[...]
    first_gain = first_gain_ref[...]
    bias = bias_ref[...]
    gain = gain_ref[...]

    def input_block(row, f):
        window_row = (place_ref[0] % BANDS) * out_rows - 1 + row
        inside = (window_row >= 0) & (window_row < out_rows * BANDS)
        taps = []
        for a in range(3):
            s, k = divmod(f + a, 3)
            for b in range(3):
                start = s * 384 + k * 16 + (row + b) * 48
                tap = planes_ref[start : start + 16, :]
                taps += [tap[:, p * 128 : (p + 1) * 128] for p in range(4)]
        patch = jnp.concatenate(taps, axis=0)
        both = lax.dot_general(
            patch, in_taps_ref[...], (((0,), (0,)), ((), ())), preferred_element_type=F32
        )
        mask = live_mask(spans, place_ref[1] + (f + 2) // 3 - 2, inside, 128)
        sides = []
        for side in range(2):
            values = both[:, side * 384 : (side + 1) * 384] + in_bias
            hidden = (values * mask).astype(BF16)
            if 1 <= row <= out_rows and f >= frames - 3:
                hidden_ref[row - 1, f - (frames - 3), side] = hidden
            sides.append(act(hidden.astype(F32), first_gain))
        at = slice(f * 128, f * 128 + 128)
        for i, part in enumerate(column_parts(*sides)):
            parts_refs[row][i, at, :] = part.astype(BF16)

    def output_block(row, f):
        at = slice(f * 128, f * 128 + 128)
        mask = live_mask(spans, place_ref[1] + (f + 1) // 3 - 1, True, 128)
        even, odd = column_sums([terms_refs[row][i, at] for i in range(4)])
        second_ref[row, 0, at] = act((odd + bias) * mask, gain).astype(BF16)
        second_ref[row, 1, at] = act((even + bias) * mask, gain).astype(BF16)

    def row_out(row):
        copy = pltpu.make_async_copy(
            second_ref.at[row], (row_0, row_1, row_2)[row], out_sems.at[row]
        )
        copy.start()
        return copy

    for f in range(frames):
        input_block(0, f)

    leaving = []
    for row in range(in_rows):
        if row < len(copies):
            for copy in copies[row]:
                copy.wait()
        for step in range(4):
            if row + 1 < in_rows:
                for f in range(2 * step, min(2 * step + 2, frames)):
                    input_block(row + 1, f)
            if row >= out_rows:
                output_block(row - out_rows, step)
            add_products(
                terms_refs,
                step,
                row,
                lambda start, n, row=row, step=step: parts_refs[row][step, start : start + n, :],
                taps_ref,
                (row,),
            )
        if row >= out_rows:
            for f in range(4, out_frames):
                output_block(row - out_rows, f)
            leaving.append(row_out(row - out_rows))
        if row == out_rows:
            copy = pltpu.make_async_copy(hidden_ref, hidden_out_ref, out_sems.at[out_rows])
            copy.start()
            leaving.append(copy)

    for f in range(out_frames):
        output_block(out_rows - 1, f)
    leaving.append(row_out(out_rows - 1))
    for copy in leaving:
        copy.wait()


def write_line(line_ref, even, odd):
    for lane in range(3):
        cut = slice(lane * 128, lane * 128 + 128)
        line_ref[lane, pl.ds(0, 64, stride=2), :] = even[:, cut]
        line_ref[lane, pl.ds(1, 64, stride=2), :] = odd[:, cut]
    return jnp.concatenate([line_ref[lane] for lane in range(3)], axis=1).astype(BF16)


def video_lives(place_ref, routing_ref, counts_ref, offsets_ref):
    spans = video_spans(place_ref, routing_ref, counts_ref, offsets_ref)
    return [
        jnp.where((place_ref[1] >= first) & (place_ref[1] < end), 1.0, 0.0) for first, end in spans
    ]


def two_lives(lives, rows):
    row = lax.broadcasted_iota(jnp.int32, (rows, 1), 0)
    return jnp.where(row < rows // 2, lives[0], lives[1])


def inner_kernel(
    place_ref,
    routing_ref,
    counts_ref,
    offsets_ref,
    row_0,
    row_1,
    row_2,
    weight_ref,
    mixed_ref,
    bias_ref,
    hidden_in_ref,
    out_ref,
    sums_out_ref,
    parts_0,
    parts_1,
    parts_2,
    taps_ref,
    terms_0,
    terms_1,
    terms_2,
    line_ref,
    hidden_ref,
    sums_ref,
    ready_ref,
    sems,
    part_sems,
    hidden_sem,
    out_sems,
):
    parts_refs = (parts_0, parts_1, parts_2)
    terms_refs = (terms_0, terms_1, terms_2)
    out_rows = len(terms_refs)
    size = terms_0.shape[1]
    out_frames = size // 128
    order = (0, 3, 1, 2)
    copies = {}
    for i in order:
        copies[i] = []
        for b in range(2):
            copies[i] += weight_copies(weight_ref, mixed_ref, taps_ref, sems, i, b)
        if i in (0, 3):
            copies[i].append(
                pltpu.make_async_copy(
                    row_0.at[min(i, 1)], parts_0.at[i], part_sems.at[0, min(i, 1)]
                )
            )
        for copy in copies[i]:
            copy.start()
    later = []
    for row, row_ref in ((1, row_1), (2, row_2)):
        for k in range(2):
            later.append(
                pltpu.make_async_copy(
                    row_ref.at[k], parts_refs[row].at[3 * k], part_sems.at[row, k]
                )
            )
    for i in order:
        later += weight_copies(weight_ref, mixed_ref, taps_ref, sems, i, 2)
    for copy in later:
        copy.start()
    hidden_copy = pltpu.make_async_copy(hidden_in_ref, hidden_ref, hidden_sem)
    hidden_copy.start()
    bias = bias_ref[...]
    live = two_lives(video_lives(place_ref, routing_ref, counts_ref, offsets_ref), 128)
    leaving = []

    def send(src, dst):
        copy = pltpu.make_async_copy(src, dst, out_sems.at[len(leaving)])
        copy.start()
        leaving.append(copy)

    def middle_parts(row):
        for f in range(parts_0.shape[1] // 128):
            at = slice(f * 128, f * 128 + 128)
            even, odd = parts_refs[row][3, at].astype(F32), parts_refs[row][0, at].astype(F32)
            parts = column_parts(even, odd)
            parts_refs[row][1, at] = parts[1].astype(BF16)
            parts_refs[row][2, at] = parts[2].astype(BF16)

    def output_block(row, f):
        at = pl.ds(pl.multiple_of(f * 128, 128), 128)
        even, odd = column_sums([terms_refs[row][i, at] for i in range(4)])
        even = (even + bias + hidden_ref[row, f, 0].astype(F32)) * live
        odd = (odd + bias + hidden_ref[row, f, 1].astype(F32)) * live
        if 0 < row < out_rows - 1:
            for video in range(2):
                here = slice(video * 64, video * 64 + 64)
                ready_ref[f, video] = write_line(line_ref.at[f, video], even[here], odd[here])
                send(ready_ref.at[f, video], out_ref.at[f, video * out_rows + row])
        else:
            side = 0 if row == 0 else 1
            sums_ref[side, 0, at] = even
            sums_ref[side, 1, at] = odd
            if f == out_frames - 1:
                send(sums_ref.at[side], sums_out_ref.at[side])

    for row in range(1, out_rows + 1):
        opening = {1: (0, 1), 2: (2,)}.get(row, ())
        if row == 2:
            for copy in later:
                copy.wait()
            hidden_copy.wait()
        for n, i in enumerate(order):
            if row == 1:
                for copy in copies[i]:
                    copy.wait()
            if n == 2:
                middle_parts(row - 1)
            add_products(
                terms_refs,
                i,
                row,
                lambda start, n, row=row, i=i: parts_refs[row - 1][i, start : start + n, :],
                taps_ref,
                opening,
            )
            if row == out_rows and n < out_frames:
                output_block(0, n)
    for row in range(1, out_rows):
        for f in range(out_frames):
            output_block(row, f)
    for copy in leaving:
        copy.wait()


def outer_kernel(
    place_ref,
    routing_ref,
    counts_ref,
    offsets_ref,
    inner_ref,
    above_ref,
    below_ref,
    weight_ref,
    mixed_ref,
    sums_ref,
    out_ref,
    edges_ref,
    taps_ref,
    sums_in_ref,
    terms_0,
    terms_1,
    line_ref,
    ready_ref,
    sems,
    out_sems,
):
    terms_refs = (terms_0, terms_1)
    size = terms_0.shape[1]
    depth = taps_ref.shape[2] // 3
    rows_per_video = out_ref.shape[1] // VPG
    copies = {}
    for side, edge_ref in enumerate((above_ref, below_ref)):
        lanes = slice(2 * side * depth, (2 * side + 1) * depth)
        for i in (0, 3, 1, 2):
            if i in (1, 2):
                moves = [(mixed_ref.at[i - 1, :, lanes], taps_ref.at[side, i])]
            else:
                column = 0 if i == 0 else 2
                moves = [
                    (
                        weight_ref.at[3 * a + 2 * side, column * depth : (column + 1) * depth, :],
                        taps_ref.at[side, i, a * depth : (a + 1) * depth, :],
                    )
                    for a in range(3)
                ]
                moves.append((edge_ref.at[0 if i == 0 else 1], edges_ref.at[side, i]))
            copies[side, i] = [
                pltpu.make_async_copy(src, dst, sems.at[side, i, n])
                for n, (src, dst) in enumerate(moves)
            ]
            for copy in copies[side, i]:
                copy.start()
        copies[side, 4] = [
            pltpu.make_async_copy(sums_ref.at[side], sums_in_ref.at[side], sems.at[side, 4, 0])
        ]
        copies[side, 4][0].start()
    live = two_lives(video_lives(place_ref, routing_ref, counts_ref, offsets_ref), 128)

    leaving = []

    def output_block(side, f):
        at = slice(f * 128, f * 128 + 128)
        even, odd = column_sums([terms_refs[side][i, at] for i in range(4)])
        even = sums_in_ref[side, 0, at] + even * live
        odd = sums_in_ref[side, 1, at] + odd * live
        for video in range(2):
            here = slice(video * 64, video * 64 + 64)
            n = len(leaving)
            ready_ref[n] = write_line(line_ref.at[n], even[here], odd[here])
            row = video * rows_per_video + side * (rows_per_video - 1)
            leaving.append(
                pltpu.make_async_copy(ready_ref.at[n], out_ref.at[f, row], out_sems.at[n])
            )
            leaving[-1].start()

    for side in range(2):
        for n, i in enumerate((0, 3, 1, 2)):
            for copy in copies[side, i]:
                copy.wait()
            if i == 1:
                even, odd = (edges_ref[side, k].astype(F32) for k in (3, 0))
                parts = column_parts(even, odd)
                edges_ref[side, 1] = parts[1].astype(BF16)
                edges_ref[side, 2] = parts[2].astype(BF16)
            stacked = jnp.concatenate(
                [edges_ref[side, i, a * 128 : a * 128 + size, :] for a in range(3)], axis=1
            )
            terms_refs[side][i] = jnp.dot(
                stacked, taps_ref[side, i], preferred_element_type=F32
            )
            if side == 1 and n < size // 128:
                output_block(0, n)
        copies[side, 4][0].wait()
    for f in range(size // 128):
        output_block(1, f)
    for copy in leaving:
        copy.wait()


SMEM = pl.BlockSpec(memory_space=pltpu.SMEM)
VMEM = pl.BlockSpec(memory_space=pltpu.VMEM)
ANY = pl.BlockSpec(memory_space=pl.ANY)


def params(limit):
    return pltpu.CompilerParams(vmem_limit_bytes=limit)


def on_device(
    latent,
    routing,
    counts,
    offsets,
    in_weight,
    in_bias,
    first_gain,
    first_weight,
    first_bias,
    second_gain,
    second_weight,
    second_bias,
):
    groups = lax.axis_size("video")
    spans = lax.axis_size("tm")
    _, span_frames, videos, window_rows, local_cols, zdim = latent.shape
    row_count = window_rows // BANDS
    channels = in_weight.shape[-1]
    pairs = groups * local_cols // 2
    span_index = lax.axis_index("tm")
    device_index = lax.axis_index("video")

    my_placed = (device_index + BANDS // 2) % groups
    place = jnp.stack([my_placed, span_index])
    scalars = (place, routing, counts, offsets)

    own = jnp.transpose(latent[0], (1, 3, 2, 0, 4))
    own = own.reshape(videos * local_cols, window_rows * span_frames * zdim)
    chunk = VPG * local_cols
    sent = pl.pallas_call(
        route_kernel,
        in_specs=[SMEM] * 4 + [VMEM],
        out_specs=VMEM,
        out_shape=jax.ShapeDtypeStruct((spans, groups * chunk, 384), BF16),
        compiler_params=pltpu.CompilerParams(vmem_limit_bytes=16 << 20),
        name="route",
    )(*scalars, own)
    sent = sent.reshape(spans * groups, chunk, 384)
    got = lax.all_to_all(sent, ("tm", "video"), 0, 0, tiled=True)
    got = got.reshape(spans, groups * chunk, 384)

    source = np.arange(groups * VPG * local_cols)
    source_col = (source // (VPG * local_cols)) * local_cols + source % local_cols
    source_video = (source // local_cols) % VPG
    pair = np.arange(pairs)
    wanted = np.stack([2 * pair - 1, 2 * pair, 2 * pair + 1, 2 * pair + 2])
    lanes = (source_col[:, None, None, None] == wanted[:, None, :]) & (
        source_video[:, None, None, None] == np.arange(VPG)[:, None]
    )
    lanes = lanes.reshape(source.size, 4 * VPG * pairs).astype(ml_dtypes.bfloat16)
    frames = 3 * span_frames
    in_frames, mid_frames = frames - 2, frames - 4
    width = VPG * pairs
    rows5_n = row_count + 2

    zero = jnp.zeros(in_weight.shape[:2] + (zdim, channels), BF16)
    in_taps = jnp.concatenate(
        [
            jnp.concatenate([in_weight, zero], axis=2),
            jnp.concatenate([zero, in_weight], axis=2),
        ],
        axis=3,
    ).reshape(-1, 2 * channels)

    depth = 3 * channels
    raw_shape = (9, depth, channels)
    edge_shape = (2, mid_frames * width, channels)
    part_shape = (4, row_count, mid_frames * width, channels)
    hidden_shape = (row_count, span_frames, 2, width, channels)
    first_raw, second_raw = first_weight.reshape(raw_shape), second_weight.reshape(raw_shape)
    first_mixed, second_mixed = mixed_weights(first_raw), mixed_weights(second_raw)
    hidden, *rows = pl.pallas_call(
        first_kernel,
        in_specs=[SMEM] * 4 + [VMEM] * 5 + [ANY] * 2 + [VMEM] * 2,
        out_specs=[ANY] * (1 + row_count),
        out_shape=[
            jax.ShapeDtypeStruct(shape, BF16) for shape in (hidden_shape, *[edge_shape] * row_count)
        ],
        scratch_shapes=[
            pltpu.VMEM((3 * 384, 4 * width), BF16),
            pltpu.VMEM((4, depth, depth), BF16),
            pltpu.VMEM(hidden_shape, BF16),
            pltpu.VMEM((row_count, *edge_shape), BF16),
            *[pltpu.VMEM((4, in_frames * width, channels), BF16)] * (row_count + 2),
            *[pltpu.VMEM((4, mid_frames * width, channels), F32)] * row_count,
            pltpu.SemaphoreType.DMA((4, 3, 3)),
            pltpu.SemaphoreType.DMA((row_count + 1,)),
        ],
        compiler_params=params(VMEM_LIMIT),
        cost_estimate=pl.CostEstimate(
            flops=25 * 10**9, bytes_accessed=24 * 10**6, transcendentals=0
        ),
        name="first_conv",
    )(
        *scalars,
        got,
        lanes,
        in_taps,
        in_bias,
        first_gain,
        first_raw,
        first_mixed,
        first_bias,
        second_gain,
    )

    above = neighbour_bands(rows[-1], "video", True)
    below = neighbour_bands(rows[0], "video", False)

    out_shape = (span_frames, VPG * row_count, 2 * pairs, channels)
    sums_shape = (2, 2, span_frames * width, channels)
    part_shape = (4, mid_frames * width, channels)
    inner, sums = pl.pallas_call(
        inner_kernel,
        in_specs=[SMEM] * 4 + [ANY] * (row_count + 2) + [VMEM, ANY],
        out_specs=[ANY, ANY],
        out_shape=[
            jax.ShapeDtypeStruct(out_shape, BF16),
            jax.ShapeDtypeStruct(sums_shape, F32),
        ],
        scratch_shapes=[
            *[pltpu.VMEM(part_shape, BF16)] * row_count,
            pltpu.VMEM((4, depth, depth), BF16),
            *[pltpu.VMEM((4, span_frames * width, channels), F32)] * row_count,
            pltpu.VMEM((span_frames, VPG, 3, 2 * pairs, 128), F32),
            pltpu.VMEM(hidden_shape, BF16),
            pltpu.VMEM(sums_shape, F32),
            pltpu.VMEM((span_frames, VPG, 2 * pairs, channels), BF16),
            pltpu.SemaphoreType.DMA((4, 3, 3)),
            pltpu.SemaphoreType.DMA((row_count, 2)),
            pltpu.SemaphoreType.DMA,
            pltpu.SemaphoreType.DMA((span_frames * VPG + 2,)),
        ],
        compiler_params=params(VMEM_LIMIT),
        cost_estimate=pl.CostEstimate(
            flops=12 * 10**9, bytes_accessed=24 * 10**6, transcendentals=0
        ),
        name="second_conv_inner",
    )(*scalars, *rows, second_raw, second_mixed, second_bias, hidden)

    edge_blocks = span_frames * 2 * VPG
    out = pl.pallas_call(
        outer_kernel,
        in_specs=[SMEM] * 4 + [ANY] * 6,
        out_specs=ANY,
        out_shape=jax.ShapeDtypeStruct(out_shape, BF16),
        input_output_aliases={4: 0},
        scratch_shapes=[
            pltpu.VMEM((2, 4, mid_frames * width, channels), BF16),
            pltpu.VMEM((2, 4, depth, channels), BF16),
            pltpu.VMEM(sums_shape, F32),
            *[pltpu.VMEM((4, span_frames * width, channels), F32)] * 2,
            pltpu.VMEM((edge_blocks, 3, 2 * pairs, 128), F32),
            pltpu.VMEM((edge_blocks, 2 * pairs, channels), BF16),
            pltpu.SemaphoreType.DMA((2, 5, 4)),
            pltpu.SemaphoreType.DMA((edge_blocks,)),
        ],
        compiler_params=params(VMEM_LIMIT),
        name="second_conv_outer",
    )(*scalars, inner, above, below, second_raw, second_mixed, sums)
    return out[None]


def solution(mesh):
    in_specs = (P("tm", None, None, None, "video", None),) + (P(),) * 11
    out_specs = P("tm", None, "video", None, None)
    return jax.shard_map(
        on_device, mesh=mesh, in_specs=in_specs, out_specs=out_specs, check_vma=False
    )
```

```python
import jax
import jax.numpy as jnp
import ml_dtypes
import numpy as np
from jax import lax
from jax.experimental import pallas as pl
from jax.experimental.pallas import tpu as pltpu
from jax.sharding import PartitionSpec as P

BANDS = 4
VPG = 2
F32 = jnp.float32
BF16 = jnp.bfloat16
VMEM_LIMIT = 60 << 20


def neighbour_bands(value, axis, down):
    count = lax.axis_size(axis)
    pairs = []
    for device in range(count):
        band = ((device + BANDS // 2) % count) % BANDS
        if down and band < BANDS - 1:
            pairs.append((device, (device + 1) % count))
        if not down and band > 0:
            pairs.append((device, (device - 1) % count))
    return lax.ppermute(value, axis, pairs)


def act(values, gain):
    scale = lax.rsqrt(jnp.mean(values * values, axis=-1, keepdims=True) + 1e-06)
    half = values * scale * (0.5 * gain)
    return half * (1.0 + jnp.tanh(half))


def column_parts(even, odd):
    return odd, even + odd, odd - even, even


def column_sums(terms):
    z0, z1, z2, z3 = terms
    rows = z0.shape[0]
    pair = lax.broadcasted_iota(jnp.int32, (rows, 1), 0) % 64
    before = jnp.where(pair == 0, 0.0, pltpu.roll(z0, 1, 0))
    after = jnp.where(pair == 63, 0.0, pltpu.roll(z3, rows - 1, 0))
    return before - z0 + (z1 + z2), after - z3 + (z1 - z2)


def route_kernel(place_ref, routing_ref, counts_ref, offsets_ref, own_ref, sent_ref):
    span_count, rows = sent_ref.shape[:2]
    lanes = own_ref.shape[0]
    span = place_ref[1]
    lane = lax.broadcasted_iota(jnp.int32, (1, lanes), 1)
    slot_of_lane = jnp.full((1, lanes), -1, jnp.int32)
    for v in range(routing_ref.shape[0]):
        live = (span >= offsets_ref[v]) & (span < offsets_ref[v] + counts_ref[v])
        slot = jnp.where(live, routing_ref[v], -1)
        slot_of_lane = jnp.where(lane // 4 == v, slot, slot_of_lane)
    row = lax.broadcasted_iota(jnp.int32, (rows, 1), 0)
    placed = (row // 8 + BANDS // 2) % (rows // 8)
    slot_of_row = (placed // BANDS) * VPG + (row // 4) % VPG
    pick = (slot_of_row == slot_of_lane) & (row % 4 == lane % 4)
    pick = jnp.where(pick, 1.0, 0.0).astype(BF16)
    moved = jnp.dot(pick, own_ref[...], preferred_element_type=F32)
    edge = jnp.zeros((rows, 96), F32)
    moved = jnp.concatenate([edge, moved, edge], axis=1)
    tail = jnp.zeros((8, 48), F32)
    reach = [jnp.where((k >= span) & (k <= span + 2), 1.0, 0.0) for k in range(span_count)]
    for pair in range(rows // 16):
        parts = []
        for device in (2 * pair, 2 * pair + 1):
            start = ((device + BANDS // 2) % BANDS) * 144
            window = moved[device * 8 : device * 8 + 8, start : start + 336]
            parts.append(jnp.concatenate([window, tail], axis=1))
        block = jnp.concatenate(parts, axis=0)
        for k in range(span_count):
            sent_ref[k, pair * 16 : pair * 16 + 16, :] = (block * reach[k]).astype(BF16)


def mix_kernel(weight_ref, out_ref, raw_ref, mixed_ref, sems, out_sems):
    taps = raw_ref.shape[0]
    depth = raw_ref.shape[1] // 3
    arriving = [
        pltpu.make_async_copy(weight_ref.at[t], raw_ref.at[t], sems.at[t]) for t in range(taps)
    ]
    for copy in arriving:
        copy.start()
    leaving = []
    for t in range(taps):
        arriving[t].wait()
        a, b = divmod(t, 3)

        def one_part(n, carry, t=t, a=a, b=b):
            g0, g1, g2 = (
                raw_ref[t, pl.ds(pl.multiple_of(k * depth + n * 64, 64), 64), :].astype(F32)
                for k in range(3)
            )
            ends = 0.5 * (g0 + g2)
            at = pl.ds(pl.multiple_of(a * depth + n * 64, 64), 64)
            mixed_ref[0, b, at] = (ends + 0.5 * g1).astype(BF16)
            mixed_ref[1, b, at] = (ends - 0.5 * g1).astype(BF16)
            return carry

        lax.fori_loop(0, depth // 64, one_part, 0)
        block = (slice(None), b, slice(a * depth, (a + 1) * depth))
        leaving.append(
            pltpu.make_async_copy(mixed_ref.at[block], out_ref.at[block], out_sems.at[t])
        )
        leaving[-1].start()
    for copy in leaving:
        copy.wait()


def mixed_weights(weight):
    taps, wide, channels = weight.shape
    depth = wide // 3
    shape = (2, 3, 3 * depth, channels)
    return pl.pallas_call(
        mix_kernel,
        in_specs=[ANY],
        out_specs=ANY,
        out_shape=jax.ShapeDtypeStruct(shape, BF16),
        scratch_shapes=[
            pltpu.VMEM(weight.shape, BF16),
            pltpu.VMEM(shape, BF16),
            pltpu.SemaphoreType.DMA((taps,)),
            pltpu.SemaphoreType.DMA((taps,)),
        ],
        compiler_params=params(VMEM_LIMIT),
        cost_estimate=pl.CostEstimate(
            flops=0, bytes_accessed=2 * weight.size + 4 * weight.size // 3, transcendentals=0
        ),
        name="mixed_weights",
    )(weight)


def weight_copies(weight_ref, mixed_ref, taps_ref, sems, which, row_tap):
    depth = taps_ref.shape[1] // 3
    lanes = slice(row_tap * depth, (row_tap + 1) * depth)
    if which in (1, 2):
        return [
            pltpu.make_async_copy(
                mixed_ref.at[which - 1, row_tap],
                taps_ref.at[which, :, lanes],
                sems.at[which, row_tap, 0],
            )
        ]
    column = 0 if which == 0 else 2
    return [
        pltpu.make_async_copy(
            weight_ref.at[3 * a + row_tap, column * depth : (column + 1) * depth, :],
            taps_ref.at[which, a * depth : (a + 1) * depth, lanes],
            sems.at[which, row_tap, a],
        )
        for a in range(3)
    ]


def video_spans(place_ref, routing_ref, counts_ref, offsets_ref):
    found = []
    for p in range(VPG):
        slot = (place_ref[0] // BANDS) * VPG + p
        first = jnp.int32(0)
        end = jnp.int32(0)
        for v in range(routing_ref.shape[0]):
            here = routing_ref[v] == slot
            first = jnp.where(here, offsets_ref[v], first)
            end = jnp.where(here, offsets_ref[v] + counts_ref[v], end)
        found.append((first, end))
    return found


def live_mask(spans, span, inside, rows):
    flags = [
        jnp.where((span >= first) & (span < end) & inside, 1.0, 0.0) for first, end in spans
    ]
    row = lax.broadcasted_iota(jnp.int32, (rows, 1), 0)
    return jnp.where(row < rows // 2, flags[0], flags[1])


def add_products(terms_refs, step, row, load, taps_ref, opening):
    size, channels = terms_refs[0].shape[1:]
    taps = [b for b in range(3) if 0 <= row - b < len(terms_refs)]
    first, last = taps[0], taps[-1] + 1
    stacked = jnp.concatenate([load(a * 128, size) for a in range(3)], axis=1)
    both = jnp.dot(
        stacked,
        taps_ref[step, :, first * channels : last * channels],
        preferred_element_type=F32,
    )
    for b in taps:
        term = both[:, (b - first) * channels : (b - first + 1) * channels]
        ref = terms_refs[row - b]
        if row - b in opening:
            ref[step] = term
        else:
            ref[step] += term


def first_kernel(
    place_ref,
    routing_ref,
    counts_ref,
    offsets_ref,
    got_ref,
    lanes_ref,
    in_taps_ref,
    in_bias_ref,
    first_gain_ref,
    weight_ref,
    mixed_ref,
    bias_ref,
    gain_ref,
    hidden_out_ref,
    row_0,
    row_1,
    row_2,
    planes_ref,
    taps_ref,
    hidden_ref,
    second_ref,
    parts_0,
    parts_1,
    parts_2,
    parts_3,
    parts_4,
    terms_0,
    terms_1,
    terms_2,
    sems,
    out_sems,
):
    parts_refs = (parts_0, parts_1, parts_2, parts_3, parts_4)
    terms_refs = (terms_0, terms_1, terms_2)
    in_rows, out_rows = len(parts_refs), len(terms_refs)
    frames = parts_0.shape[1] // 128
    out_frames = terms_0.shape[1] // 128
    copies = [
        [
            copy
            for which in range(4)
            for copy in weight_copies(weight_ref, mixed_ref, taps_ref, sems, which, b)
        ]
        for b in range(3)
    ]
    for column in copies:
        for copy in column:
            copy.start()
    spans = video_spans(place_ref, routing_ref, counts_ref, offsets_ref)
    span_count = got_ref.shape[0]
    for k in range(3):
        span = (place_ref[1] + span_count - 2 + k) % span_count
        planes_ref[k * 384 : (k + 1) * 384, :] = lax.dot_general(
            got_ref[span], lanes_ref[...], (((0,), (0,)), ((), ())), preferred_element_type=F32
        ).astype(BF16)
    in_bias = in_bias_ref[...]
    first_gain = first_gain_ref[...]
    bias = bias_ref[...]
    gain = gain_ref[...]

    def input_block(row, f):
        window_row = (place_ref[0] % BANDS) * out_rows - 1 + row
        inside = (window_row >= 0) & (window_row < out_rows * BANDS)
        taps = []
        for a in range(3):
            s, k = divmod(f + a, 3)
            for b in range(3):
                start = s * 384 + k * 16 + (row + b) * 48
                tap = planes_ref[start : start + 16, :]
                taps += [tap[:, p * 128 : (p + 1) * 128] for p in range(4)]
        patch = jnp.concatenate(taps, axis=0)
        both = lax.dot_general(
            patch, in_taps_ref[...], (((0,), (0,)), ((), ())), preferred_element_type=F32
        )
        mask = live_mask(spans, place_ref[1] + (f + 2) // 3 - 2, inside, 128)
        sides = []
        for side in range(2):
            values = both[:, side * 384 : (side + 1) * 384] + in_bias
            hidden = (values * mask).astype(BF16)
            if 1 <= row <= out_rows and f >= frames - 3:
                hidden_ref[row - 1, f - (frames - 3), side] = hidden
            sides.append(act(hidden.astype(F32), first_gain))
        at = slice(f * 128, f * 128 + 128)
        for i, part in enumerate(column_parts(*sides)):
            parts_refs[row][i, at, :] = part.astype(BF16)

    def output_block(row, f):
        at = slice(f * 128, f * 128 + 128)
        mask = live_mask(spans, place_ref[1] + (f + 1) // 3 - 1, True, 128)
        even, odd = column_sums([terms_refs[row][i, at] for i in range(4)])
        second_ref[row, 0, at] = act((odd + bias) * mask, gain).astype(BF16)
        second_ref[row, 1, at] = act((even + bias) * mask, gain).astype(BF16)

    def row_out(row):
        copy = pltpu.make_async_copy(
            second_ref.at[row], (row_0, row_1, row_2)[row], out_sems.at[row]
        )
        copy.start()
        return copy

    for f in range(frames):
        input_block(0, f)

    leaving = []
    for row in range(in_rows):
        for b in {0: (0,), 1: (1, 2)}.get(row, ()):
            for copy in copies[b]:
                copy.wait()
        for step in range(4):
            if row + 1 < in_rows:
                for f in range(2 * step, min(2 * step + 2, frames)):
                    input_block(row + 1, f)
            if row >= out_rows:
                output_block(row - out_rows, step)
            add_products(
                terms_refs,
                step,
                row,
                lambda start, n, row=row, step=step: parts_refs[row][step, start : start + n, :],
                taps_ref,
                (row,),
            )
        if row >= out_rows:
            for f in range(4, out_frames):
                output_block(row - out_rows, f)
            leaving.append(row_out(row - out_rows))
        if row == out_rows:
            copy = pltpu.make_async_copy(hidden_ref, hidden_out_ref, out_sems.at[out_rows])
            copy.start()
            leaving.append(copy)

    for f in range(out_frames):
        output_block(out_rows - 1, f)
    leaving.append(row_out(out_rows - 1))
    for copy in leaving:
        copy.wait()


def write_line(line_ref, even, odd):
    for lane in range(3):
        cut = slice(lane * 128, lane * 128 + 128)
        line_ref[lane, pl.ds(0, 64, stride=2), :] = even[:, cut]
        line_ref[lane, pl.ds(1, 64, stride=2), :] = odd[:, cut]
    return jnp.concatenate([line_ref[lane] for lane in range(3)], axis=1).astype(BF16)


def video_lives(place_ref, routing_ref, counts_ref, offsets_ref):
    spans = video_spans(place_ref, routing_ref, counts_ref, offsets_ref)
    return [
        jnp.where((place_ref[1] >= first) & (place_ref[1] < end), 1.0, 0.0) for first, end in spans
    ]


def two_lives(lives, rows):
    row = lax.broadcasted_iota(jnp.int32, (rows, 1), 0)
    return jnp.where(row < rows // 2, lives[0], lives[1])


def inner_kernel(
    place_ref,
    routing_ref,
    counts_ref,
    offsets_ref,
    row_0,
    row_1,
    row_2,
    weight_ref,
    mixed_ref,
    bias_ref,
    hidden_in_ref,
    out_ref,
    sums_out_ref,
    parts_0,
    parts_1,
    parts_2,
    taps_ref,
    terms_0,
    terms_1,
    terms_2,
    line_ref,
    hidden_ref,
    sums_ref,
    ready_ref,
    sems,
    part_sems,
    hidden_sem,
    out_sems,
):
    parts_refs = (parts_0, parts_1, parts_2)
    terms_refs = (terms_0, terms_1, terms_2)
    out_rows = len(terms_refs)
    size = terms_0.shape[1]
    out_frames = size // 128
    order = (0, 3, 1, 2)
    copies = {}
    for i in order:
        copies[i] = []
        for b in range(2):
            copies[i] += weight_copies(weight_ref, mixed_ref, taps_ref, sems, i, b)
        if i in (0, 3):
            copies[i].append(
                pltpu.make_async_copy(
                    row_0.at[min(i, 1)], parts_0.at[i], part_sems.at[0, min(i, 1)]
                )
            )
        for copy in copies[i]:
            copy.start()
    later = []
    for row, row_ref in ((1, row_1), (2, row_2)):
        for k in range(2):
            later.append(
                pltpu.make_async_copy(
                    row_ref.at[k], parts_refs[row].at[3 * k], part_sems.at[row, k]
                )
            )
    for i in order:
        later += weight_copies(weight_ref, mixed_ref, taps_ref, sems, i, 2)
    for copy in later:
        copy.start()
    hidden_copy = pltpu.make_async_copy(hidden_in_ref, hidden_ref, hidden_sem)
    hidden_copy.start()
    bias = bias_ref[...]
    live = two_lives(video_lives(place_ref, routing_ref, counts_ref, offsets_ref), 128)
    leaving = []

    def send(src, dst):
        copy = pltpu.make_async_copy(src, dst, out_sems.at[len(leaving)])
        copy.start()
        leaving.append(copy)

    def middle_parts(row):
        for f in range(parts_0.shape[1] // 128):
            at = slice(f * 128, f * 128 + 128)
            even, odd = parts_refs[row][3, at].astype(F32), parts_refs[row][0, at].astype(F32)
            parts = column_parts(even, odd)
            parts_refs[row][1, at] = parts[1].astype(BF16)
            parts_refs[row][2, at] = parts[2].astype(BF16)

    def output_block(row, f):
        at = pl.ds(pl.multiple_of(f * 128, 128), 128)
        even, odd = column_sums([terms_refs[row][i, at] for i in range(4)])
        even = (even + bias + hidden_ref[row, f, 0].astype(F32)) * live
        odd = (odd + bias + hidden_ref[row, f, 1].astype(F32)) * live
        if 0 < row < out_rows - 1:
            for video in range(2):
                here = slice(video * 64, video * 64 + 64)
                ready_ref[f, video] = write_line(line_ref.at[f, video], even[here], odd[here])
                send(ready_ref.at[f, video], out_ref.at[f, video * out_rows + row])
        else:
            side = 0 if row == 0 else 1
            sums_ref[side, 0, at] = even
            sums_ref[side, 1, at] = odd
            if f == out_frames - 1:
                send(sums_ref.at[side], sums_out_ref.at[side])

    for row in range(1, out_rows + 1):
        opening = {1: (0, 1), 2: (2,)}.get(row, ())
        if row == 2:
            for copy in later:
                copy.wait()
            hidden_copy.wait()
        for n, i in enumerate(order):
            if row == 1 and n % 2 == 0:
                for copy in copies[i] + copies[order[n + 1]]:
                    copy.wait()
            if n == 2:
                middle_parts(row - 1)
            add_products(
                terms_refs,
                i,
                row,
                lambda start, n, row=row, i=i: parts_refs[row - 1][i, start : start + n, :],
                taps_ref,
                opening,
            )
            if row == out_rows and n < out_frames:
                output_block(0, n)
    for row in range(1, out_rows):
        for f in range(out_frames):
            output_block(row, f)
    for copy in leaving:
        copy.wait()


def outer_kernel(
    place_ref,
    routing_ref,
    counts_ref,
    offsets_ref,
    inner_ref,
    above_ref,
    below_ref,
    weight_ref,
    mixed_ref,
    sums_ref,
    out_ref,
    edges_ref,
    taps_ref,
    sums_in_ref,
    terms_0,
    terms_1,
    line_ref,
    ready_ref,
    sems,
    out_sems,
):
    terms_refs = (terms_0, terms_1)
    size = terms_0.shape[1]
    depth = taps_ref.shape[2] // 3
    rows_per_video = out_ref.shape[1] // VPG
    copies = {}
    for side, edge_ref in enumerate((above_ref, below_ref)):
        for i in (0, 3, 1, 2):
            if i in (1, 2):
                moves = [(mixed_ref.at[i - 1, 2 * side], taps_ref.at[side, i])]
            else:
                column = 0 if i == 0 else 2
                moves = [
                    (
                        weight_ref.at[3 * a + 2 * side, column * depth : (column + 1) * depth, :],
                        taps_ref.at[side, i, a * depth : (a + 1) * depth, :],
                    )
                    for a in range(3)
                ]
                moves.append((edge_ref.at[0 if i == 0 else 1], edges_ref.at[side, i]))
            copies[side, i] = [
                pltpu.make_async_copy(src, dst, sems.at[side, i, n])
                for n, (src, dst) in enumerate(moves)
            ]
            for copy in copies[side, i]:
                copy.start()
        copies[side, 4] = [
            pltpu.make_async_copy(sums_ref.at[side], sums_in_ref.at[side], sems.at[side, 4, 0])
        ]
        copies[side, 4][0].start()
    live = two_lives(video_lives(place_ref, routing_ref, counts_ref, offsets_ref), 128)

    leaving = []

    def output_block(side, f):
        at = slice(f * 128, f * 128 + 128)
        even, odd = column_sums([terms_refs[side][i, at] for i in range(4)])
        even = sums_in_ref[side, 0, at] + even * live
        odd = sums_in_ref[side, 1, at] + odd * live
        for video in range(2):
            here = slice(video * 64, video * 64 + 64)
            n = len(leaving)
            ready_ref[n] = write_line(line_ref.at[n], even[here], odd[here])
            row = video * rows_per_video + side * (rows_per_video - 1)
            leaving.append(
                pltpu.make_async_copy(ready_ref.at[n], out_ref.at[f, row], out_sems.at[n])
            )
            leaving[-1].start()

    for side in range(2):
        for n, i in enumerate((0, 3, 1, 2)):
            if n % 2 == 0:
                for copy in copies[side, i] + copies[side, (3, 2)[n // 2]]:
                    copy.wait()
            if i == 1:
                even, odd = (edges_ref[side, k].astype(F32) for k in (3, 0))
                parts = column_parts(even, odd)
                edges_ref[side, 1] = parts[1].astype(BF16)
                edges_ref[side, 2] = parts[2].astype(BF16)
            stacked = jnp.concatenate(
                [edges_ref[side, i, a * 128 : a * 128 + size, :] for a in range(3)], axis=1
            )
            terms_refs[side][i] = jnp.dot(
                stacked, taps_ref[side, i], preferred_element_type=F32
            )
            if side == 1 and n < size // 128:
                output_block(0, n)
        copies[side, 4][0].wait()
    for f in range(size // 128):
        output_block(1, f)
    for copy in leaving:
        copy.wait()


SMEM = pl.BlockSpec(memory_space=pltpu.SMEM)
VMEM = pl.BlockSpec(memory_space=pltpu.VMEM)
ANY = pl.BlockSpec(memory_space=pl.ANY)


def params(limit):
    return pltpu.CompilerParams(vmem_limit_bytes=limit)


def on_device(
    latent,
    routing,
    counts,
    offsets,
    in_weight,
    in_bias,
    first_gain,
    first_weight,
    first_bias,
    second_gain,
    second_weight,
    second_bias,
):
    groups = lax.axis_size("video")
    spans = lax.axis_size("tm")
    _, span_frames, videos, window_rows, local_cols, zdim = latent.shape
    row_count = window_rows // BANDS
    channels = in_weight.shape[-1]
    pairs = groups * local_cols // 2
    span_index = lax.axis_index("tm")
    device_index = lax.axis_index("video")

    my_placed = (device_index + BANDS // 2) % groups
    place = jnp.stack([my_placed, span_index])
    scalars = (place, routing, counts, offsets)

    own = jnp.transpose(latent[0], (1, 3, 2, 0, 4))
    own = own.reshape(videos * local_cols, window_rows * span_frames * zdim)
    chunk = VPG * local_cols
    sent = pl.pallas_call(
        route_kernel,
        in_specs=[SMEM] * 4 + [VMEM],
        out_specs=VMEM,
        out_shape=jax.ShapeDtypeStruct((spans, groups * chunk, 384), BF16),
        compiler_params=pltpu.CompilerParams(vmem_limit_bytes=16 << 20),
        name="route",
    )(*scalars, own)
    sent = sent.reshape(spans * groups, chunk, 384)
    got = lax.all_to_all(sent, ("tm", "video"), 0, 0, tiled=True)
    got = got.reshape(spans, groups * chunk, 384)

    source = np.arange(groups * VPG * local_cols)
    source_col = (source // (VPG * local_cols)) * local_cols + source % local_cols
    source_video = (source // local_cols) % VPG
    pair = np.arange(pairs)
    wanted = np.stack([2 * pair - 1, 2 * pair, 2 * pair + 1, 2 * pair + 2])
    lanes = (source_col[:, None, None, None] == wanted[:, None, :]) & (
        source_video[:, None, None, None] == np.arange(VPG)[:, None]
    )
    lanes = lanes.reshape(source.size, 4 * VPG * pairs).astype(ml_dtypes.bfloat16)
    frames = 3 * span_frames
    in_frames, mid_frames = frames - 2, frames - 4
    width = VPG * pairs
    rows5_n = row_count + 2

    zero = jnp.zeros(in_weight.shape[:2] + (zdim, channels), BF16)
    in_taps = jnp.concatenate(
        [
            jnp.concatenate([in_weight, zero], axis=2),
            jnp.concatenate([zero, in_weight], axis=2),
        ],
        axis=3,
    ).reshape(-1, 2 * channels)

    depth = 3 * channels
    raw_shape = (9, depth, channels)
    edge_shape = (2, mid_frames * width, channels)
    part_shape = (4, row_count, mid_frames * width, channels)
    hidden_shape = (row_count, span_frames, 2, width, channels)
    first_raw, second_raw = first_weight.reshape(raw_shape), second_weight.reshape(raw_shape)
    first_mixed, second_mixed = mixed_weights(first_raw), mixed_weights(second_raw)
    hidden, *rows = pl.pallas_call(
        first_kernel,
        in_specs=[SMEM] * 4 + [VMEM] * 5 + [ANY] * 2 + [VMEM] * 2,
        out_specs=[ANY] * (1 + row_count),
        out_shape=[
            jax.ShapeDtypeStruct(shape, BF16) for shape in (hidden_shape, *[edge_shape] * row_count)
        ],
        scratch_shapes=[
            pltpu.VMEM((3 * 384, 4 * width), BF16),
            pltpu.VMEM((4, depth, depth), BF16),
            pltpu.VMEM(hidden_shape, BF16),
            pltpu.VMEM((row_count, *edge_shape), BF16),
            *[pltpu.VMEM((4, in_frames * width, channels), BF16)] * (row_count + 2),
            *[pltpu.VMEM((4, mid_frames * width, channels), F32)] * row_count,
            pltpu.SemaphoreType.DMA((4, 3, 3)),
            pltpu.SemaphoreType.DMA((row_count + 1,)),
        ],
        compiler_params=params(VMEM_LIMIT),
        cost_estimate=pl.CostEstimate(
            flops=25 * 10**9, bytes_accessed=24 * 10**6, transcendentals=0
        ),
        name="first_conv",
    )(
        *scalars,
        got,
        lanes,
        in_taps,
        in_bias,
        first_gain,
        first_raw,
        first_mixed,
        first_bias,
        second_gain,
    )

    above = neighbour_bands(rows[-1], "video", True)
    below = neighbour_bands(rows[0], "video", False)

    out_shape = (span_frames, VPG * row_count, 2 * pairs, channels)
    sums_shape = (2, 2, span_frames * width, channels)
    part_shape = (4, mid_frames * width, channels)
    inner, sums = pl.pallas_call(
        inner_kernel,
        in_specs=[SMEM] * 4 + [ANY] * (row_count + 2) + [VMEM, ANY],
        out_specs=[ANY, ANY],
        out_shape=[
            jax.ShapeDtypeStruct(out_shape, BF16),
            jax.ShapeDtypeStruct(sums_shape, F32),
        ],
        scratch_shapes=[
            *[pltpu.VMEM(part_shape, BF16)] * row_count,
            pltpu.VMEM((4, depth, depth), BF16),
            *[pltpu.VMEM((4, span_frames * width, channels), F32)] * row_count,
            pltpu.VMEM((span_frames, VPG, 3, 2 * pairs, 128), F32),
            pltpu.VMEM(hidden_shape, BF16),
            pltpu.VMEM(sums_shape, F32),
            pltpu.VMEM((span_frames, VPG, 2 * pairs, channels), BF16),
            pltpu.SemaphoreType.DMA((4, 3, 3)),
            pltpu.SemaphoreType.DMA((row_count, 2)),
            pltpu.SemaphoreType.DMA,
            pltpu.SemaphoreType.DMA((span_frames * VPG + 2,)),
        ],
        compiler_params=params(VMEM_LIMIT),
        cost_estimate=pl.CostEstimate(
            flops=12 * 10**9, bytes_accessed=24 * 10**6, transcendentals=0
        ),
        name="second_conv_inner",
    )(*scalars, *rows, second_raw, second_mixed, second_bias, hidden)

    edge_blocks = span_frames * 2 * VPG
    out = pl.pallas_call(
        outer_kernel,
        in_specs=[SMEM] * 4 + [ANY] * 6,
        out_specs=ANY,
        out_shape=jax.ShapeDtypeStruct(out_shape, BF16),
        input_output_aliases={4: 0},
        scratch_shapes=[
            pltpu.VMEM((2, 4, mid_frames * width, channels), BF16),
            pltpu.VMEM((2, 4, depth, channels), BF16),
            pltpu.VMEM(sums_shape, F32),
            *[pltpu.VMEM((4, span_frames * width, channels), F32)] * 2,
            pltpu.VMEM((edge_blocks, 3, 2 * pairs, 128), F32),
            pltpu.VMEM((edge_blocks, 2 * pairs, channels), BF16),
            pltpu.SemaphoreType.DMA((2, 5, 4)),
            pltpu.SemaphoreType.DMA((edge_blocks,)),
        ],
        compiler_params=params(VMEM_LIMIT),
        name="second_conv_outer",
    )(*scalars, inner, above, below, second_raw, second_mixed, sums)
    return out[None]


def solution(mesh):
    in_specs = (P("tm", None, None, None, "video", None),) + (P(),) * 11
    out_specs = P("tm", None, "video", None, None)
    return jax.shard_map(
        on_device, mesh=mesh, in_specs=in_specs, out_specs=out_specs, check_vma=False
    )
```

```python
import jax
import jax.numpy as jnp
import ml_dtypes
import numpy as np
from jax import lax
from jax.experimental import pallas as pl
from jax.experimental.pallas import tpu as pltpu
from jax.sharding import PartitionSpec as P

BANDS = 4
VPG = 2
F32 = jnp.float32
BF16 = jnp.bfloat16
VMEM_LIMIT = 60 << 20
VMEM_MOST = (64 << 20) - (256 << 10)


def neighbour_bands(value, axis, down):
    count = lax.axis_size(axis)
    pairs = []
    for device in range(count):
        band = ((device + BANDS // 2) % count) % BANDS
        if down and band < BANDS - 1:
            pairs.append((device, (device + 1) % count))
        if not down and band > 0:
            pairs.append((device, (device - 1) % count))
    return lax.ppermute(value, axis, pairs)


def act(values, gain):
    scale = lax.rsqrt(jnp.mean(values * values, axis=-1, keepdims=True) + 1e-06)
    half = values * scale * (0.5 * gain)
    return half * (1.0 + jnp.tanh(half))


def column_parts(even, odd):
    return odd, even + odd, odd - even, even


def column_sums(terms):
    z0, z1, z2, z3 = terms
    rows = z0.shape[0]
    pair = lax.broadcasted_iota(jnp.int32, (rows, 1), 0) % 64
    before = jnp.where(pair == 0, 0.0, pltpu.roll(z0, 1, 0))
    after = jnp.where(pair == 63, 0.0, pltpu.roll(z3, rows - 1, 0))
    return before - z0 + (z1 + z2), after - z3 + (z1 - z2)


def route_kernel(place_ref, routing_ref, counts_ref, offsets_ref, own_ref, sent_ref):
    span_count, rows = sent_ref.shape[:2]
    lanes = own_ref.shape[0]
    span = place_ref[1]
    lane = lax.broadcasted_iota(jnp.int32, (1, lanes), 1)
    slot_of_lane = jnp.full((1, lanes), -1, jnp.int32)
    for v in range(routing_ref.shape[0]):
        live = (span >= offsets_ref[v]) & (span < offsets_ref[v] + counts_ref[v])
        slot = jnp.where(live, routing_ref[v], -1)
        slot_of_lane = jnp.where(lane // 4 == v, slot, slot_of_lane)
    row = lax.broadcasted_iota(jnp.int32, (rows, 1), 0)
    placed = (row // 8 + BANDS // 2) % (rows // 8)
    slot_of_row = (placed // BANDS) * VPG + (row // 4) % VPG
    pick = (slot_of_row == slot_of_lane) & (row % 4 == lane % 4)
    pick = jnp.where(pick, 1.0, 0.0).astype(BF16)
    moved = jnp.dot(pick, own_ref[...], preferred_element_type=F32)
    edge = jnp.zeros((rows, 96), F32)
    moved = jnp.concatenate([edge, moved, edge], axis=1)
    tail = jnp.zeros((8, 48), F32)
    reach = [jnp.where((k >= span) & (k <= span + 2), 1.0, 0.0) for k in range(span_count)]
    for pair in range(rows // 16):
        parts = []
        for device in (2 * pair, 2 * pair + 1):
            start = ((device + BANDS // 2) % BANDS) * 144
            window = moved[device * 8 : device * 8 + 8, start : start + 336]
            parts.append(jnp.concatenate([window, tail], axis=1))
        block = jnp.concatenate(parts, axis=0)
        for k in range(span_count):
            sent_ref[k, pair * 16 : pair * 16 + 16, :] = (block * reach[k]).astype(BF16)


def mix_kernel(weight_ref, out_ref, raw_ref, mixed_ref, sems, out_sems):
    taps = raw_ref.shape[0]
    depth = raw_ref.shape[1] // 3
    arriving = [
        pltpu.make_async_copy(weight_ref.at[t], raw_ref.at[t], sems.at[t]) for t in range(taps)
    ]
    for copy in arriving:
        copy.start()
    leaving = []
    for t in range(taps):
        arriving[t].wait()
        a, b = divmod(t, 3)
        lanes = slice(b * depth, (b + 1) * depth)

        def one_part(n, carry, t=t, a=a, lanes=lanes):
            g0, g1, g2 = (
                raw_ref[t, pl.ds(pl.multiple_of(k * depth + n * 64, 64), 64), :].astype(F32)
                for k in range(3)
            )
            ends = 0.5 * (g0 + g2)
            at = pl.ds(pl.multiple_of(a * depth + n * 64, 64), 64)
            mixed_ref[0, at, lanes] = (ends + 0.5 * g1).astype(BF16)
            mixed_ref[1, at, lanes] = (ends - 0.5 * g1).astype(BF16)
            return carry

        lax.fori_loop(0, depth // 64, one_part, 0)
        block = (slice(None), slice(a * depth, (a + 1) * depth), lanes)
        leaving.append(
            pltpu.make_async_copy(mixed_ref.at[block], out_ref.at[block], out_sems.at[t])
        )
        leaving[-1].start()
    for copy in leaving:
        copy.wait()


def mixed_weights(weight):
    taps, wide, channels = weight.shape
    depth = wide // 3
    shape = (2, 3 * depth, 3 * channels)
    return pl.pallas_call(
        mix_kernel,
        in_specs=[ANY],
        out_specs=ANY,
        out_shape=jax.ShapeDtypeStruct(shape, BF16),
        scratch_shapes=[
            pltpu.VMEM(weight.shape, BF16),
            pltpu.VMEM(shape, BF16),
            pltpu.SemaphoreType.DMA((taps,)),
            pltpu.SemaphoreType.DMA((taps,)),
        ],
        compiler_params=params(VMEM_LIMIT),
        cost_estimate=pl.CostEstimate(
            flops=0, bytes_accessed=2 * weight.size + 4 * weight.size // 3, transcendentals=0
        ),
        name="mixed_weights",
    )(weight)


def weight_copies(weight_ref, mixed_ref, taps_ref, sems, which, row_tap):
    depth = taps_ref.shape[1] // 3
    lanes = slice(row_tap * depth, (row_tap + 1) * depth)
    if which in (1, 2):
        return [
            pltpu.make_async_copy(
                mixed_ref.at[which - 1, :, lanes],
                taps_ref.at[which, :, lanes],
                sems.at[which, row_tap, 0],
            )
        ]
    column = 0 if which == 0 else 2
    return [
        pltpu.make_async_copy(
            weight_ref.at[3 * a + row_tap, column * depth : (column + 1) * depth, :],
            taps_ref.at[which, a * depth : (a + 1) * depth, lanes],
            sems.at[which, row_tap, a],
        )
        for a in range(3)
    ]


def video_spans(place_ref, routing_ref, counts_ref, offsets_ref):
    found = []
    for p in range(VPG):
        slot = (place_ref[0] // BANDS) * VPG + p
        first = jnp.int32(0)
        end = jnp.int32(0)
        for v in range(routing_ref.shape[0]):
            here = routing_ref[v] == slot
            first = jnp.where(here, offsets_ref[v], first)
            end = jnp.where(here, offsets_ref[v] + counts_ref[v], end)
        found.append((first, end))
    return found


def live_mask(spans, span, inside, rows):
    flags = [
        jnp.where((span >= first) & (span < end) & inside, 1.0, 0.0) for first, end in spans
    ]
    row = lax.broadcasted_iota(jnp.int32, (rows, 1), 0)
    return jnp.where(row < rows // 2, flags[0], flags[1])


def add_products(terms_refs, step, row, load, taps_ref, opening):
    size, channels = terms_refs[0].shape[1:]
    taps = [b for b in range(3) if 0 <= row - b < len(terms_refs)]
    first, last = taps[0], taps[-1] + 1
    stacked = jnp.concatenate([load(a * 128, size) for a in range(3)], axis=1)
    both = jnp.dot(
        stacked,
        taps_ref[step, :, first * channels : last * channels],
        preferred_element_type=F32,
    )
    for b in taps:
        term = both[:, (b - first) * channels : (b - first + 1) * channels]
        ref = terms_refs[row - b]
        if row - b in opening:
            ref[step] = term
        else:
            ref[step] += term


def first_kernel(
    place_ref,
    routing_ref,
    counts_ref,
    offsets_ref,
    got_ref,
    lanes_ref,
    in_taps_ref,
    in_bias_ref,
    first_gain_ref,
    weight_ref,
    mixed_ref,
    bias_ref,
    gain_ref,
    hidden_out_ref,
    row_0,
    row_1,
    row_2,
    planes_ref,
    taps_ref,
    hidden_ref,
    second_ref,
    parts_0,
    parts_1,
    parts_2,
    parts_3,
    parts_4,
    terms_0,
    terms_1,
    terms_2,
    sems,
    out_sems,
):
    parts_refs = (parts_0, parts_1, parts_2, parts_3, parts_4)
    terms_refs = (terms_0, terms_1, terms_2)
    in_rows, out_rows = len(parts_refs), len(terms_refs)
    frames = parts_0.shape[1] // 128
    out_frames = terms_0.shape[1] // 128
    copies = [
        [
            copy
            for which in range(4)
            for copy in weight_copies(weight_ref, mixed_ref, taps_ref, sems, which, b)
        ]
        for b in range(3)
    ]
    for column in copies:
        for copy in column:
            copy.start()
    spans = video_spans(place_ref, routing_ref, counts_ref, offsets_ref)
    span_count = got_ref.shape[0]
    for k in range(3):
        span = (place_ref[1] + span_count - 2 + k) % span_count
        planes_ref[k * 384 : (k + 1) * 384, :] = lax.dot_general(
            got_ref[span], lanes_ref[...], (((0,), (0,)), ((), ())), preferred_element_type=F32
        ).astype(BF16)
    in_bias = in_bias_ref[...]
    first_gain = first_gain_ref[...]
    bias = bias_ref[...]
    gain = gain_ref[...]

    def input_block(row, f):
        window_row = (place_ref[0] % BANDS) * out_rows - 1 + row
        inside = (window_row >= 0) & (window_row < out_rows * BANDS)
        taps = []
        for a in range(3):
            s, k = divmod(f + a, 3)
            for b in range(3):
                start = s * 384 + k * 16 + (row + b) * 48
                tap = planes_ref[start : start + 16, :]
                taps += [tap[:, p * 128 : (p + 1) * 128] for p in range(4)]
        patch = jnp.concatenate(taps, axis=0)
        both = lax.dot_general(
            patch, in_taps_ref[...], (((0,), (0,)), ((), ())), preferred_element_type=F32
        )
        mask = live_mask(spans, place_ref[1] + (f + 2) // 3 - 2, inside, 128)
        sides = []
        for side in range(2):
            values = both[:, side * 384 : (side + 1) * 384] + in_bias
            hidden = (values * mask).astype(BF16)
            if 1 <= row <= out_rows and f >= frames - 3:
                hidden_ref[row - 1, f - (frames - 3), side] = hidden
            sides.append(act(hidden.astype(F32), first_gain))
        at = slice(f * 128, f * 128 + 128)
        for i, part in enumerate(column_parts(*sides)):
            parts_refs[row][i, at, :] = part.astype(BF16)

    def output_block(row, f):
        at = slice(f * 128, f * 128 + 128)
        mask = live_mask(spans, place_ref[1] + (f + 1) // 3 - 1, True, 128)
        even, odd = column_sums([terms_refs[row][i, at] for i in range(4)])
        second_ref[row, 0, at] = act((odd + bias) * mask, gain).astype(BF16)
        second_ref[row, 1, at] = act((even + bias) * mask, gain).astype(BF16)

    def row_out(row):
        copy = pltpu.make_async_copy(
            second_ref.at[row], (row_0, row_1, row_2)[row], out_sems.at[row]
        )
        copy.start()
        return copy

    for f in range(frames):
        input_block(0, f)

    leaving = []
    for row in range(in_rows):
        if row < len(copies):
            for copy in copies[row]:
                copy.wait()
        for step in range(4):
            if row + 1 < in_rows:
                for f in range(2 * step, min(2 * step + 2, frames)):
                    input_block(row + 1, f)
            if row >= out_rows:
                output_block(row - out_rows, step)
            add_products(
                terms_refs,
                step,
                row,
                lambda start, n, row=row, step=step: parts_refs[row][step, start : start + n, :],
                taps_ref,
                (row,),
            )
        if row >= out_rows:
            for f in range(4, out_frames):
                output_block(row - out_rows, f)
            leaving.append(row_out(row - out_rows))
        if row == out_rows:
            copy = pltpu.make_async_copy(hidden_ref, hidden_out_ref, out_sems.at[out_rows])
            copy.start()
            leaving.append(copy)

    for f in range(out_frames):
        output_block(out_rows - 1, f)
    leaving.append(row_out(out_rows - 1))
    for copy in leaving:
        copy.wait()


def write_line(line_ref, even, odd):
    for lane in range(3):
        cut = slice(lane * 128, lane * 128 + 128)
        line_ref[lane, pl.ds(0, 64, stride=2), :] = even[:, cut]
        line_ref[lane, pl.ds(1, 64, stride=2), :] = odd[:, cut]
    return jnp.concatenate([line_ref[lane] for lane in range(3)], axis=1).astype(BF16)


def video_lives(place_ref, routing_ref, counts_ref, offsets_ref):
    spans = video_spans(place_ref, routing_ref, counts_ref, offsets_ref)
    return [
        jnp.where((place_ref[1] >= first) & (place_ref[1] < end), 1.0, 0.0) for first, end in spans
    ]


def two_lives(lives, rows):
    row = lax.broadcasted_iota(jnp.int32, (rows, 1), 0)
    return jnp.where(row < rows // 2, lives[0], lives[1])


def inner_kernel(
    place_ref,
    routing_ref,
    counts_ref,
    offsets_ref,
    row_0,
    row_1,
    row_2,
    weight_ref,
    mixed_ref,
    bias_ref,
    hidden_in_ref,
    out_ref,
    sums_out_ref,
    parts_0,
    parts_1,
    parts_2,
    taps_ref,
    terms_0,
    terms_1,
    terms_2,
    line_ref,
    hidden_ref,
    sums_ref,
    ready_ref,
    sems,
    part_sems,
    hidden_sem,
    out_sems,
):
    parts_refs = (parts_0, parts_1, parts_2)
    terms_refs = (terms_0, terms_1, terms_2)
    out_rows = len(terms_refs)
    size = terms_0.shape[1]
    out_frames = size // 128
    order = (0, 3, 1, 2)
    copies = {}
    for i in order:
        copies[i] = []
        for b in range(2):
            copies[i] += weight_copies(weight_ref, mixed_ref, taps_ref, sems, i, b)
        if i in (0, 3):
            copies[i].append(
                pltpu.make_async_copy(
                    row_0.at[min(i, 1)], parts_0.at[i], part_sems.at[0, min(i, 1)]
                )
            )
        for copy in copies[i]:
            copy.start()
    later = []
    for row, row_ref in ((1, row_1), (2, row_2)):
        for k in range(2):
            later.append(
                pltpu.make_async_copy(
                    row_ref.at[k], parts_refs[row].at[3 * k], part_sems.at[row, k]
                )
            )
    for i in order:
        later += weight_copies(weight_ref, mixed_ref, taps_ref, sems, i, 2)
    for copy in later:
        copy.start()
    hidden_copy = pltpu.make_async_copy(hidden_in_ref, hidden_ref, hidden_sem)
    hidden_copy.start()
    bias = bias_ref[...]
    live = two_lives(video_lives(place_ref, routing_ref, counts_ref, offsets_ref), 128)
    leaving = []

    def send(src, dst):
        copy = pltpu.make_async_copy(src, dst, out_sems.at[len(leaving)])
        copy.start()
        leaving.append(copy)

    def middle_parts(row):
        for f in range(parts_0.shape[1] // 128):
            at = slice(f * 128, f * 128 + 128)
            even, odd = parts_refs[row][3, at].astype(F32), parts_refs[row][0, at].astype(F32)
            parts = column_parts(even, odd)
            parts_refs[row][1, at] = parts[1].astype(BF16)
            parts_refs[row][2, at] = parts[2].astype(BF16)

    def output_block(row, f):
        at = pl.ds(pl.multiple_of(f * 128, 128), 128)
        even, odd = column_sums([terms_refs[row][i, at] for i in range(4)])
        even = (even + bias + hidden_ref[row, f, 0].astype(F32)) * live
        odd = (odd + bias + hidden_ref[row, f, 1].astype(F32)) * live
        if 0 < row < out_rows - 1:
            for video in range(2):
                here = slice(video * 64, video * 64 + 64)
                ready_ref[f, video] = write_line(line_ref.at[f, video], even[here], odd[here])
                send(ready_ref.at[f, video], out_ref.at[f, video * out_rows + row])
        else:
            side = 0 if row == 0 else 1
            sums_ref[side, 0, at] = even
            sums_ref[side, 1, at] = odd
            if f == out_frames - 1:
                send(sums_ref.at[side], sums_out_ref.at[side])

    for row in range(1, out_rows + 1):
        opening = {1: (0, 1), 2: (2,)}.get(row, ())
        if row == 2:
            for copy in later:
                copy.wait()
            hidden_copy.wait()
        for n, i in enumerate(order):
            if row == 1:
                for copy in copies[i]:
                    copy.wait()
            if n == 2:
                middle_parts(row - 1)
            add_products(
                terms_refs,
                i,
                row,
                lambda start, n, row=row, i=i: parts_refs[row - 1][i, start : start + n, :],
                taps_ref,
                opening,
            )
            if row == out_rows and n < out_frames:
                output_block(0, n)
    for row in range(1, out_rows):
        for f in range(out_frames):
            output_block(row, f)
    for copy in leaving:
        copy.wait()


def outer_kernel(
    place_ref,
    routing_ref,
    counts_ref,
    offsets_ref,
    inner_ref,
    above_ref,
    below_ref,
    weight_ref,
    mixed_ref,
    sums_ref,
    out_ref,
    edges_ref,
    taps_ref,
    sums_in_ref,
    terms_0,
    terms_1,
    line_ref,
    ready_ref,
    sems,
    out_sems,
):
    terms_refs = (terms_0, terms_1)
    size = terms_0.shape[1]
    depth = taps_ref.shape[2] // 3
    rows_per_video = out_ref.shape[1] // VPG
    copies = {}
    for side, edge_ref in enumerate((above_ref, below_ref)):
        lanes = slice(2 * side * depth, (2 * side + 1) * depth)
        for i in (0, 3, 1, 2):
            if i in (1, 2):
                moves = [(mixed_ref.at[i - 1, :, lanes], taps_ref.at[side, i])]
            else:
                column = 0 if i == 0 else 2
                moves = [
                    (
                        weight_ref.at[3 * a + 2 * side, column * depth : (column + 1) * depth, :],
                        taps_ref.at[side, i, a * depth : (a + 1) * depth, :],
                    )
                    for a in range(3)
                ]
                moves.append((edge_ref.at[0 if i == 0 else 1], edges_ref.at[side, i]))
            copies[side, i] = [
                pltpu.make_async_copy(src, dst, sems.at[side, i, n])
                for n, (src, dst) in enumerate(moves)
            ]
            for copy in copies[side, i]:
                copy.start()
        copies[side, 4] = [
            pltpu.make_async_copy(sums_ref.at[side], sums_in_ref.at[side], sems.at[side, 4, 0])
        ]
        copies[side, 4][0].start()
    live = two_lives(video_lives(place_ref, routing_ref, counts_ref, offsets_ref), 128)

    leaving = []

    def output_block(side, f):
        at = slice(f * 128, f * 128 + 128)
        even, odd = column_sums([terms_refs[side][i, at] for i in range(4)])
        even = sums_in_ref[side, 0, at] + even * live
        odd = sums_in_ref[side, 1, at] + odd * live
        for video in range(2):
            here = slice(video * 64, video * 64 + 64)
            n = len(leaving)
            ready_ref[n] = write_line(line_ref.at[n], even[here], odd[here])
            row = video * rows_per_video + side * (rows_per_video - 1)
            leaving.append(
                pltpu.make_async_copy(ready_ref.at[n], out_ref.at[f, row], out_sems.at[n])
            )
            leaving[-1].start()

    for side in range(2):
        for n, i in enumerate((0, 3, 1, 2)):
            if n % 2 == 0:
                for copy in copies[side, i] + copies[side, (3, 2)[n // 2]]:
                    copy.wait()
            if i == 1:
                even, odd = (edges_ref[side, k].astype(F32) for k in (3, 0))
                parts = column_parts(even, odd)
                edges_ref[side, 1] = parts[1].astype(BF16)
                edges_ref[side, 2] = parts[2].astype(BF16)
            stacked = jnp.concatenate(
                [edges_ref[side, i, a * 128 : a * 128 + size, :] for a in range(3)], axis=1
            )
            terms_refs[side][i] = jnp.dot(
                stacked, taps_ref[side, i], preferred_element_type=F32
            )
            if side == 1 and n < size // 128:
                output_block(0, n)
        copies[side, 4][0].wait()
    for f in range(size // 128):
        output_block(1, f)
    for copy in leaving:
        copy.wait()


SMEM = pl.BlockSpec(memory_space=pltpu.SMEM)
VMEM = pl.BlockSpec(memory_space=pltpu.VMEM)
ANY = pl.BlockSpec(memory_space=pl.ANY)


def params(limit):
    return pltpu.CompilerParams(vmem_limit_bytes=limit)


def on_device(
    latent,
    routing,
    counts,
    offsets,
    in_weight,
    in_bias,
    first_gain,
    first_weight,
    first_bias,
    second_gain,
    second_weight,
    second_bias,
):
    groups = lax.axis_size("video")
    spans = lax.axis_size("tm")
    _, span_frames, videos, window_rows, local_cols, zdim = latent.shape
    row_count = window_rows // BANDS
    channels = in_weight.shape[-1]
    pairs = groups * local_cols // 2
    span_index = lax.axis_index("tm")
    device_index = lax.axis_index("video")

    my_placed = (device_index + BANDS // 2) % groups
    place = jnp.stack([my_placed, span_index])
    scalars = (place, routing, counts, offsets)

    own = jnp.transpose(latent[0], (1, 3, 2, 0, 4))
    own = own.reshape(videos * local_cols, window_rows * span_frames * zdim)
    chunk = VPG * local_cols
    sent = pl.pallas_call(
        route_kernel,
        in_specs=[SMEM] * 4 + [VMEM],
        out_specs=VMEM,
        out_shape=jax.ShapeDtypeStruct((spans, groups * chunk, 384), BF16),
        compiler_params=pltpu.CompilerParams(vmem_limit_bytes=16 << 20),
        name="route",
    )(*scalars, own)
    sent = sent.reshape(spans * groups, chunk, 384)
    got = lax.all_to_all(sent, ("tm", "video"), 0, 0, tiled=True)
    got = got.reshape(spans, groups * chunk, 384)

    source = np.arange(groups * VPG * local_cols)
    source_col = (source // (VPG * local_cols)) * local_cols + source % local_cols
    source_video = (source // local_cols) % VPG
    pair = np.arange(pairs)
    wanted = np.stack([2 * pair - 1, 2 * pair, 2 * pair + 1, 2 * pair + 2])
    lanes = (source_col[:, None, None, None] == wanted[:, None, :]) & (
        source_video[:, None, None, None] == np.arange(VPG)[:, None]
    )
    lanes = lanes.reshape(source.size, 4 * VPG * pairs).astype(ml_dtypes.bfloat16)
    frames = 3 * span_frames
    in_frames, mid_frames = frames - 2, frames - 4
    width = VPG * pairs
    rows5_n = row_count + 2

    zero = jnp.zeros(in_weight.shape[:2] + (zdim, channels), BF16)
    in_taps = jnp.concatenate(
        [
            jnp.concatenate([in_weight, zero], axis=2),
            jnp.concatenate([zero, in_weight], axis=2),
        ],
        axis=3,
    ).reshape(-1, 2 * channels)

    depth = 3 * channels
    raw_shape = (9, depth, channels)
    edge_shape = (2, mid_frames * width, channels)
    part_shape = (4, row_count, mid_frames * width, channels)
    hidden_shape = (row_count, span_frames, 2, width, channels)
    first_raw, second_raw = first_weight.reshape(raw_shape), second_weight.reshape(raw_shape)
    first_mixed, second_mixed = mixed_weights(first_raw), mixed_weights(second_raw)
    hidden, *rows = pl.pallas_call(
        first_kernel,
        in_specs=[SMEM] * 4 + [VMEM] * 5 + [ANY] * 2 + [VMEM] * 2,
        out_specs=[ANY] * (1 + row_count),
        out_shape=[
            jax.ShapeDtypeStruct(shape, BF16) for shape in (hidden_shape, *[edge_shape] * row_count)
        ],
        scratch_shapes=[
            pltpu.VMEM((3 * 384, 4 * width), BF16),
            pltpu.VMEM((4, depth, depth), BF16),
            pltpu.VMEM(hidden_shape, BF16),
            pltpu.VMEM((row_count, *edge_shape), BF16),
            *[pltpu.VMEM((4, in_frames * width, channels), BF16)] * (row_count + 2),
            *[pltpu.VMEM((4, mid_frames * width, channels), F32)] * row_count,
            pltpu.SemaphoreType.DMA((4, 3, 3)),
            pltpu.SemaphoreType.DMA((row_count + 1,)),
        ],
        compiler_params=params(VMEM_LIMIT),
        cost_estimate=pl.CostEstimate(
            flops=25 * 10**9, bytes_accessed=24 * 10**6, transcendentals=0
        ),
        name="first_conv",
    )(
        *scalars,
        got,
        lanes,
        in_taps,
        in_bias,
        first_gain,
        first_raw,
        first_mixed,
        first_bias,
        second_gain,
    )

    above = neighbour_bands(rows[-1], "video", True)
    below = neighbour_bands(rows[0], "video", False)

    out_shape = (span_frames, VPG * row_count, 2 * pairs, channels)
    sums_shape = (2, 2, span_frames * width, channels)
    part_shape = (4, mid_frames * width, channels)
    inner, sums = pl.pallas_call(
        inner_kernel,
        in_specs=[SMEM] * 4 + [ANY] * (row_count + 2) + [VMEM, ANY],
        out_specs=[ANY, ANY],
        out_shape=[
            jax.ShapeDtypeStruct(out_shape, BF16),
            jax.ShapeDtypeStruct(sums_shape, F32),
        ],
        scratch_shapes=[
            *[pltpu.VMEM(part_shape, BF16)] * row_count,
            pltpu.VMEM((4, depth, depth), BF16),
            *[pltpu.VMEM((4, span_frames * width, channels), F32)] * row_count,
            pltpu.VMEM((span_frames, VPG, 3, 2 * pairs, 128), F32),
            pltpu.VMEM(hidden_shape, BF16),
            pltpu.VMEM(sums_shape, F32),
            pltpu.VMEM((span_frames, VPG, 2 * pairs, channels), BF16),
            pltpu.SemaphoreType.DMA((4, 3, 3)),
            pltpu.SemaphoreType.DMA((row_count, 2)),
            pltpu.SemaphoreType.DMA,
            pltpu.SemaphoreType.DMA((span_frames * VPG + 2,)),
        ],
        compiler_params=params(VMEM_MOST),
        cost_estimate=pl.CostEstimate(
            flops=12 * 10**9, bytes_accessed=24 * 10**6, transcendentals=0
        ),
        name="second_conv_inner",
    )(*scalars, *rows, second_raw, second_mixed, second_bias, hidden)

    edge_blocks = span_frames * 2 * VPG
    out = pl.pallas_call(
        outer_kernel,
        in_specs=[SMEM] * 4 + [ANY] * 6,
        out_specs=ANY,
        out_shape=jax.ShapeDtypeStruct(out_shape, BF16),
        input_output_aliases={4: 0},
        scratch_shapes=[
            pltpu.VMEM((2, 4, mid_frames * width, channels), BF16),
            pltpu.VMEM((2, 4, depth, channels), BF16),
            pltpu.VMEM(sums_shape, F32),
            *[pltpu.VMEM((4, span_frames * width, channels), F32)] * 2,
            pltpu.VMEM((edge_blocks, 3, 2 * pairs, 128), F32),
            pltpu.VMEM((edge_blocks, 2 * pairs, channels), BF16),
            pltpu.SemaphoreType.DMA((2, 5, 4)),
            pltpu.SemaphoreType.DMA((edge_blocks,)),
        ],
        compiler_params=params(VMEM_MOST),
        name="second_conv_outer",
    )(*scalars, inner, above, below, second_raw, second_mixed, sums)
    return out[None]


def solution(mesh):
    in_specs = (P("tm", None, None, None, "video", None),) + (P(),) * 11
    out_specs = P("tm", None, "video", None, None)
    return jax.shard_map(
        on_device, mesh=mesh, in_specs=in_specs, out_specs=out_specs, check_vma=False
    )
```
